32 devices in a mesh: ctx: 8 (over y, x, core), tp: 4 (over z).
Axes of the slice: x: 2, y: 2, z: 4, core: 2. Of those that a mesh axis runs over, the one named last changes fastest.
Arguments:
- tokens: bfloat16 [2048, 2304], P('ctx'), may hold values from -6 to 6
- w_query: bfloat16 [2304, 2048], P('ctx', 'tp'), may hold values from -0.375 to 0.375
- w_key: bfloat16 [2304, 1024], P('ctx', 'tp'), may hold values from -0.125 to 0.125
- w_value: bfloat16 [2304, 1024], P('ctx', 'tp'), may hold values from -0.125 to 0.125
- w_out: bfloat16 [2304, 2048], P('ctx', 'tp'), may hold values from -0.125 to 0.125
- w_gate: bfloat16 [2304, 9216], P('ctx', 'tp'), may hold values from -0.125 to 0.125
- w_up: bfloat16 [2304, 9216], P('ctx', 'tp'), may hold values from -0.125 to 0.125
- w_down: bfloat16 [2304, 9216], P('ctx', 'tp'), may hold values from -0.0625 to 0.0625
- norm_attn_in: bfloat16 [2304], P('ctx'), may hold values from 0.099609375 to 1.8984375
- norm_attn_out: bfloat16 [2304], P('ctx'), may hold values from 0.099609375 to 1.8984375
- norm_ffn_in: bfloat16 [2304], P('ctx'), may hold values from 0.099609375 to 1.8984375
- norm_ffn_out: bfloat16 [2304], P('ctx'), may hold values from 0.099609375 to 1.8984375
- cotangent: bfloat16 [2048, 2304], P('ctx'), may hold values from -6 to 6
Outputs:
- output: bfloat16 [2048, 2304], P('ctx')
- grad_tokens: float32 [2048, 2304], P('ctx')
- grad_w_query: float32 [2304, 2048], P('ctx', 'tp')
- grad_w_key: float32 [2304, 1024], P('ctx', 'tp')
- grad_w_value: float32 [2304, 1024], P('ctx', 'tp')
- grad_w_out: float32 [2304, 2048], P('ctx', 'tp')
- grad_w_gate: float32 [2304, 9216], P('ctx', 'tp')
- grad_w_up: float32 [2304, 9216], P('ctx', 'tp')
- grad_w_down: float32 [2304, 9216], P('ctx', 'tp')
- grad_norm_attn_in: float32 [2304], P('ctx')
- grad_norm_attn_out: float32 [2304], P('ctx')
- grad_norm_ffn_in: float32 [2304], P('ctx')
- grad_norm_ffn_out: float32 [2304], P('ctx')
The draws below stay inside these ranges and needn't reach their ends.
All inputs are finite; a program needn't handle non-finite values.
Results may differ from the reference program's by a relative error of at most 0.028.
Values may be sent and summed in bfloat16 or wider, within the bound.
No kernel may reach another device: no remote copies, remote signals or barrier semaphores. Data moves between devices by JAX's collectives and lax.ppermute only.
A program may use at most 256 MiB of HBM per device.

```python
import math
import jax
import jax.numpy as jnp
from jax import lax

D = 2304
H = 8
KVH = 4
HD = 256
FF = 9216
SEQ = 2048


def strengthened(entries, stream_key, source, target, parts, factor):
    def block_of(dim):
        return (jnp.arange(entries.shape[dim]) // (entries.shape[dim] // parts)).reshape((-1,) + (1,) * (entries.ndim - 1 - dim))

    first = jax.random.permutation(stream_key, parts)[block_of(target)]
    second = (block_of(target) + parts // 2) % parts
    return jnp.where((block_of(source) == first) | (block_of(source) == second), factor * entries, entries)


def shard_levels(own_key, dims, cuts, least, top_value):
    def one(dim, parts):
        heights = jax.random.uniform(jax.random.fold_in(jax.random.fold_in(own_key, 6), dim), (parts,), jnp.float32, least / len(cuts), top_value / len(cuts))
        return jnp.repeat(jnp.exp(heights), dims[dim] // parts).reshape((-1,) + (1,) * (len(dims) - dim - 1))

    loudness = one(*cuts[0])
    for cut in cuts[1:]:
        loudness = loudness * one(*cut)
    return loudness


def noise(own_key, dims, scale, most, cuts=(), kind=jnp.bfloat16):
    loudness = shard_levels(own_key, dims, cuts, -0.22, 0.18) if cuts else 1.0
    values = jax.random.normal(own_key, dims, jnp.float32) * scale * loudness
    return jnp.minimum(jnp.maximum(values, -most), most).astype(kind)


def heavy_noise(rng, extent, spread, most, split, heavy, held_as=jnp.bfloat16):
    result = spread * jax.random.normal(rng, extent, jnp.float32)
    if split:
        result = result * shard_levels(rng, extent, split, -0.22, 0.18)
    return jnp.clip(strengthened(result, jax.random.fold_in(rng, 3), *heavy), -most, most).astype(held_as)


def setup_inputs(seed: int = 0) -> dict:
    arg_keys = jax.random.split(jax.random.key(seed), 14)
    tokens = noise(arg_keys[0], (SEQ, D), 1.0, 6.0, ((0, 8),))
    w_query = noise(arg_keys[1], (D, H * HD), (D // 9) ** -0.5, 0.375, ((0, 8), (1, 4)))
    w_key = noise(arg_keys[2], (D, KVH * HD), D ** -0.5, 0.125, ((0, 8), (1, 4)))
    w_value = noise(arg_keys[3], (D, KVH * HD), D ** -0.5, 0.125, ((0, 8), (1, 4)))
    w_out = noise(arg_keys[4], (D, H * HD), (H * HD) ** -0.5, 0.125, ((0, 8), (1, 4)))
    w_gate = noise(arg_keys[5], (D, FF), D ** -0.5, 0.125, ((0, 8), (1, 4)))
    w_up = noise(arg_keys[6], (D, FF), D ** -0.5, 0.125, ((0, 8), (1, 4)))
    w_down = noise(arg_keys[7], (D, FF), FF ** -0.5, 0.0625, ((0, 8), (1, 4)))
    norm_attn_in = jnp.clip(1.0 + 0.18 * jax.random.normal(arg_keys[8], (D,), jnp.float32), 0.099609375, 1.8984375).astype(jnp.bfloat16)
    norm_attn_out = jnp.clip(1.0 + 0.18 * jax.random.normal(arg_keys[9], (D,), jnp.float32), 0.099609375, 1.8984375).astype(jnp.bfloat16)
    norm_ffn_in = jnp.clip(1.0 + 0.18 * jax.random.normal(arg_keys[10], (D,), jnp.float32), 0.099609375, 1.8984375).astype(jnp.bfloat16)
    norm_ffn_out = jnp.clip(1.0 + 0.18 * jax.random.normal(arg_keys[11], (D,), jnp.float32), 0.099609375, 1.8984375).astype(jnp.bfloat16)
    cotangent = heavy_noise(arg_keys[12], (SEQ, D), 1.0, 6.0, ((0, 8),), (0, 1, 8, 2.0))
    return dict(tokens=tokens, w_query=w_query, w_key=w_key, w_value=w_value, w_out=w_out, w_gate=w_gate, w_up=w_up, w_down=w_down, norm_attn_in=norm_attn_in, norm_attn_out=norm_attn_out, norm_ffn_in=norm_ffn_in, norm_ffn_out=norm_ffn_out, cotangent=cotangent)


EPSILON = 1e-06
SOFT_CAP = 50.0
MASKED = -1e+30
HIGHEST = lax.Precision.HIGHEST

@jax.custom_vjp
def low(v):
    return lax.optimization_barrier(v.astype(jnp.bfloat16)).astype(jnp.float32)

@jax.custom_vjp
def low_back(v):
    return v

def low_keep(v):
    return (low(v), None)

def low_pass(kept, grad):
    return (grad,)

def back_keep(v):
    return (v, None)

def back_low(kept, grad):
    return (low(grad),)
low.defvjp(low_keep, low_pass)
low_back.defvjp(back_keep, back_low)

def rms_scale(values):
    return lax.rsqrt(lax.optimization_barrier(jnp.mean(values * values, axis=-1, keepdims=True)) + EPSILON)

def rope_tables(row_count, head_width):
    half_width = head_width // 2
    positions = jnp.arange(row_count, dtype=jnp.int32).astype(jnp.float32)
    frequency = jnp.exp(jnp.arange(half_width, dtype=jnp.float32) * (-2.0 * math.log(10000.0) / head_width))
    angles = positions[:, None] * frequency[None, :]
    return (jnp.cos(angles)[:, None, :], jnp.sin(angles)[:, None, :])

def rotate(values, cos_table, sine_table):
    half_width = values.shape[-1] // 2
    leading = values[..., :half_width]
    trailing = values[..., half_width:]
    return jnp.concatenate([leading * cos_table - trailing * sine_table, trailing * cos_table + leading * sine_table], axis=-1)

def product(first_operand, second_operand):
    return jnp.dot(first_operand, second_operand, precision=HIGHEST, preferred_element_type=jnp.float32)

def forward(tokens, w_query, w_key, w_value, w_out, w_gate, w_up, w_down, gain_one, gain_two, gain_three, gain_four):
    length = tokens.shape[0]
    attn_in = low(tokens * rms_scale(tokens) * gain_one)
    cos_table, sine_table = rope_tables(length, HD)
    query_lin = low_back(product(attn_in, w_query)).reshape(length, H, HD)
    key_lin = low_back(product(attn_in, w_key)).reshape(length, KVH, HD)
    values = low(low_back(product(attn_in, w_value))).reshape(length, KVH, HD)
    queries = low(rotate(query_lin, cos_table, sine_table) * HD ** (-0.5))
    keys_rot = low(rotate(key_lin, cos_table, sine_table))
    keys_full = jnp.repeat(keys_rot, H // KVH, axis=1)
    values_full = jnp.repeat(values, H // KVH, axis=1)
    block_rows = math.gcd(length, 512)
    count_blocks = length // block_rows
    key_pos = jnp.arange(length, dtype=jnp.int32)

    def one_block(inputs):
        query_block, block_index = inputs
        query_pos = block_index * block_rows + jnp.arange(block_rows, dtype=jnp.int32)
        raw_scores = low_back(jnp.einsum('qhd,khd->hqk', query_block, keys_full, precision=HIGHEST))
        capped = SOFT_CAP * jnp.tanh(raw_scores / SOFT_CAP)
        visible = key_pos[None, :] <= query_pos[:, None]
        capped = jnp.where(visible[None], capped, MASKED)
        row_top = lax.optimization_barrier(jnp.max(capped, axis=-1, keepdims=True))
        weights = jnp.exp(capped - row_top)
        probability = weights / lax.optimization_barrier(jnp.sum(weights, axis=-1, keepdims=True))
        return jnp.einsum('hqk,khd->qhd', low(probability), values_full, precision=HIGHEST)
    attended = lax.map(jax.checkpoint(one_block), (queries.reshape(count_blocks, block_rows, H, HD), jnp.arange(count_blocks, dtype=jnp.int32)))
    attn_rows = low(low_back(attended.reshape(length, H * HD)))
    attn_proj = low_back(product(attn_rows, w_out.T))
    hidden_res = tokens + attn_proj * rms_scale(attn_proj) * gain_two
    ffn_in = low(hidden_res * rms_scale(hidden_res) * gain_three)
    gate_lin = low_back(product(ffn_in, w_gate))
    up_lin = low_back(product(ffn_in, w_up))
    hidden = low(jax.nn.gelu(gate_lin, approximate=True) * up_lin)
    ffn_proj = low_back(product(hidden, w_down.T))
    return hidden_res + ffn_proj * rms_scale(ffn_proj) * gain_four

def reference(tokens, w_query, w_key, w_value, w_out, w_gate, w_up, w_down, norm_attn_in, norm_attn_out, norm_ffn_in, norm_ffn_out, cotangent):
    floats = tuple((array.astype(jnp.float32) for array in (tokens, w_query, w_key, w_value, w_out, w_gate, w_up, w_down, norm_attn_in, norm_attn_out, norm_ffn_in, norm_ffn_out)))
    output, pullback = jax.vjp(forward, *floats)
    gradients = pullback(cotangent.astype(jnp.float32))
    return (output.astype(jnp.bfloat16), gradients[0], gradients[1], gradients[2], gradients[3], gradients[4], gradients[5], gradients[6], gradients[7], gradients[8], gradients[9], gradients[10], gradients[11])
```

```python
import math

import jax
import jax.numpy as jnp
from jax import lax
from jax.sharding import PartitionSpec as P

HD = 256


EPSILON = 1e-06
SOFT_CAP = 50.0
MASKED = -1e30


def rms_scale(values):
    return lax.rsqrt(jnp.mean(values * values, axis=-1, keepdims=True) + EPSILON)


def norm_back(inv_rms, normed, gradient):
    return inv_rms * (gradient - normed * jnp.mean(gradient * normed, axis=-1, keepdims=True))


def rotate(values, cos_table, sine_table):
    half_width = values.shape[-1] // 2
    leading = values[..., :half_width]
    trailing = values[..., half_width:]
    return jnp.concatenate(
        [leading * cos_table - trailing * sine_table, trailing * cos_table + leading * sine_table],
        axis=-1,
    )


def gelu_tanh(values):
    return jax.nn.gelu(values, approximate=True)


def product(first_operand, second_operand):
    return jnp.dot(first_operand, second_operand, preferred_element_type=jnp.float32)


def contract(first_operand, second_operand, first_dim, second_dim):
    return lax.dot_general(
        first_operand,
        second_operand,
        (((first_dim,), (second_dim,)), ((), ())),
        preferred_element_type=jnp.float32,
    )


def after(value, *earlier):
    return lax.optimization_barrier((value,) + earlier)[0]


def local(
    tokens,
    w_query,
    w_key,
    w_value,
    w_out,
    w_gate,
    w_up,
    w_down,
    norm_attn_in,
    norm_attn_out,
    norm_ffn_in,
    norm_ffn_out,
    cotangent,
):
    bf16, f32 = jnp.bfloat16, jnp.float32
    tok_rows, width = tokens.shape
    heads_local = w_query.shape[1] // HD
    key_heads = w_key.shape[1] // HD
    group_size = heads_local // key_heads
    query_width = heads_local * HD
    key_width = key_heads * HD
    ring = lax.axis_size("ctx")
    layers = lax.axis_size("tp")
    me = lax.axis_index("ctx")
    my_layer = lax.axis_index("tp")
    shard = width // ring
    own_rows = tok_rows // layers
    far_a, far_b = ring // 4, ring // 2
    near = [1 << bit for bit in range(far_a.bit_length() - 1)]
    order = [0, far_a, far_b, far_a | far_b]
    for bit in near:
        order = order + [block | bit for block in order]

    def swap(value, bit, axis="ctx"):
        count = lax.axis_size(axis)
        return lax.ppermute(value, axis, [(index, index ^ bit) for index in range(count)])

    def spread_far(piece):
        cut = piece.shape[0] // 32 * 16
        from_a, from_b = swap(piece, far_a), swap(piece, far_b)
        top, bottom = swap(from_b[:cut], far_a), swap(from_a[cut:], far_b)
        return jnp.concatenate([piece, from_a, from_b, top, bottom], axis=0), (from_a, from_b)

    def spread_near(block):
        blocks = [block]
        for bit in near:
            blocks = blocks + [swap(held, bit) for held in blocks]
        return blocks

    def collect_near(parts):
        for bit in reversed(near):
            half = len(parts) // 2
            parts = [
                (kept.astype(f32) + swap(sent, bit).astype(f32)).astype(bf16)
                for kept, sent in zip(parts[:half], parts[half:])
            ]
        return parts[0]

    def collect_far(block):
        rows = block.shape[0] // 4
        cut = rows // 32 * 16
        own, for_a, for_b, for_ab = (block[index * rows : (index + 1) * rows] for index in range(4))
        top, bottom = swap(for_ab[:cut], far_a), swap(for_ab[cut:], far_b)
        for_b = jnp.concatenate(
            [(for_b[:cut].astype(f32) + top.astype(f32)).astype(bf16), for_b[cut:]], axis=0
        )
        for_a = jnp.concatenate(
            [for_a[:cut], (for_a[cut:].astype(f32) + bottom.astype(f32)).astype(bf16)], axis=0
        )
        return own.astype(f32) + swap(for_a, far_a).astype(f32) + swap(for_b, far_b).astype(f32)

    def layer_scatter(partial):
        total = partial[:own_rows].astype(f32)
        arrived = [
            swap(partial[step * own_rows : (step + 1) * own_rows], step, "tp")
            for step in range(1, layers)
        ]
        for piece in arrived:
            total = total + piece.astype(f32)
        return total

    def layer_gather(rows):
        return [rows] + [swap(rows, step, "tp") for step in range(1, layers)]

    def rows_in(array):
        return jnp.concatenate(
            [
                lax.dynamic_slice_in_dim(array, (my_layer ^ step) * own_rows, own_rows, 0)
                for step in range(layers)
            ],
            axis=0,
        )

    def columns_in(array):
        return jnp.concatenate(
            [lax.dynamic_slice_in_dim(array, (me ^ block) * shard, shard, 1) for block in order],
            axis=1,
        )

    def columns_out(array):
        result = jnp.zeros_like(array)
        for place, block in enumerate(order):
            result = lax.dynamic_update_slice_in_dim(
                result, array[:, place * shard : (place + 1) * shard], (me ^ block) * shard, 1
            )
        return result

    def rows_out(pieces):
        result = jnp.zeros((tok_rows,) + pieces[0].shape[1:], pieces[0].dtype)
        for step, piece in enumerate(pieces):
            result = lax.dynamic_update_slice_in_dim(
                result, piece, (my_layer ^ step) * own_rows, 0
            )
        return result

    near_count = len(order) // 4
    near_width = 4 * shard

    def by_near(array):
        return [
            array[:, index * near_width : (index + 1) * near_width] for index in range(near_count)
        ]

    def times_rows(activation, blocks):
        total = None
        for part, block in zip(by_near(activation), blocks):
            term = product(part, block)
            total = term if total is None else total + term
        return total

    def times_rows_t(activation, blocks):
        return jnp.concatenate([contract(activation, block, 1, 1) for block in blocks], axis=1)

    def weight_parts(activation, gradient):
        return [
            contract(part, gradient, 0, 0).astype(bf16) for part in by_near(activation)
        ]

    gains = jnp.stack([norm_attn_in, norm_attn_out, norm_ffn_in, norm_ffn_out])
    qkv_width = query_width + 2 * key_width
    qkv = jnp.concatenate([w_query, w_key, w_value], axis=1)
    gain_rows = jnp.zeros((16, qkv_width), bf16).at[:4, :shard].set(gains)
    qkv_far, qkv_done = spread_far(jnp.concatenate([qkv, gain_rows], axis=0))
    out_far, out_done = spread_far(w_out)
    gate_far, gate_done = spread_far(after(w_gate, *out_done))
    up_far, up_done = spread_far(after(w_up, *gate_done))
    down_far, _ = spread_far(after(w_down, *up_done))
    qkv_all = spread_near(qkv_far)
    out_all = spread_near(out_far)
    gate_all = spread_near(gate_far)
    up_all = spread_near(up_far)
    down_all = spread_near(down_far)
    padded = shard + 16
    qkv_all_rows = [block.reshape(4, padded, qkv_width) for block in qkv_all]
    qkv_w = [block[:, :shard].reshape(near_width, qkv_width) for block in qkv_all_rows]
    gain_all = jnp.concatenate(
        [block[index, shard : shard + 4, :shard] for block in qkv_all_rows for index in range(4)],
        axis=1,
    ).astype(f32)
    gain_one, gain_two, gain_three, gain_four = (gain_all[index : index + 1] for index in range(4))

    tok_float = columns_in(rows_in(tokens)).astype(f32)
    own_cot = columns_in(
        lax.dynamic_slice_in_dim(cotangent, my_layer * own_rows, own_rows, 0)
    ).astype(f32)
    attn_input = (tok_float * rms_scale(tok_float) * gain_one).astype(bf16)
    own_tok = tok_float[:own_rows]
    lin = times_rows(attn_input, qkv_w)
    row_place = jnp.concatenate(
        [
            (my_layer ^ step) * own_rows + jnp.arange(own_rows, dtype=jnp.int32)
            for step in range(layers)
        ]
    )
    query_pos = me * tok_rows + row_place
    half_width = HD // 2
    frequency = jnp.exp(
        jnp.arange(half_width, dtype=f32) * (-2.0 * math.log(10000.0) / HD)
    )
    angles = query_pos.astype(f32)[:, None] * frequency[None, :]
    cos_table, sine_table = jnp.cos(angles)[:, None, :], jnp.sin(angles)[:, None, :]
    queries = (
        rotate(lin[:, :query_width].reshape(tok_rows, heads_local, HD), cos_table, sine_table)
        * HD ** (-0.5)
    ).astype(bf16)
    queries_h = queries.reshape(tok_rows, key_heads, group_size, HD).transpose(1, 2, 0, 3)
    keys_rot = (
        rotate(
            lin[:, query_width : query_width + key_width].reshape(tok_rows, key_heads, HD),
            cos_table,
            sine_table,
        )
        .astype(bf16)
        .reshape(tok_rows, key_width)
    )
    values_b = lin[:, query_width + key_width :].astype(bf16)
    pair = jnp.concatenate([keys_rot, values_b], axis=1)
    pair_far = jnp.concatenate(
        [pair, swap(pair, far_a), swap(pair, far_b), swap(pair, far_a | far_b)], axis=0
    )
    pairs = jnp.concatenate(spread_near(pair_far), axis=0)
    key_count = pairs.shape[0]
    key_h = pairs[:, :key_width].reshape(key_count, key_heads, HD)
    value_h = pairs[:, key_width:].reshape(key_count, key_heads, HD)
    key_pos = jnp.concatenate([(me ^ block) * tok_rows + row_place for block in order])
    visible = key_pos[None, :] <= query_pos[:, None]
    tanh_part = jnp.tanh(
        jnp.einsum("jgqd,cjd->jgqc", queries_h, key_h, preferred_element_type=f32) / SOFT_CAP
    )
    capped = jnp.where(visible, SOFT_CAP * tanh_part, MASKED)
    row_max = jnp.max(capped, axis=-1)
    weights = jnp.where(visible, jnp.exp(capped - row_max[..., None]), 0.0)
    row_sum = jnp.sum(weights, axis=-1)
    attn_float = (
        jnp.einsum("jgqc,cjd->jgqd", weights.astype(bf16), value_h, preferred_element_type=f32)
        / row_sum[..., None]
    )
    log_total = row_max + jnp.log(row_sum)
    attn_rows = attn_float.transpose(2, 0, 1, 3).reshape(tok_rows, query_width).astype(bf16)
    attn_total = layer_scatter(times_rows_t(attn_rows, out_all).astype(bf16))
    inv_two = rms_scale(attn_total)
    normed_two = attn_total * inv_two
    hidden_res = own_tok + normed_two * gain_two
    inv_three = rms_scale(hidden_res)
    normed_three = hidden_res * inv_three
    ffn_input = jnp.concatenate(
        layer_gather((normed_three * gain_three).astype(bf16)), axis=0
    )

    gate_lin = times_rows(ffn_input, gate_all)
    up_lin = times_rows(ffn_input, up_all)
    activated, gelu_pull = jax.vjp(gelu_tanh, gate_lin)
    hidden_b = (activated * up_lin).astype(bf16)
    ffn_total = layer_scatter(times_rows_t(hidden_b, down_all).astype(bf16))
    inv_four = rms_scale(ffn_total)
    normed_four = ffn_total * inv_four
    own_output = (hidden_res + normed_four * gain_four).astype(bf16)
    output = rows_out(layer_gather(columns_out(own_output)))

    grad_gain_four = jnp.sum(own_cot * normed_four, axis=0)
    grad_ffn = jnp.concatenate(
        layer_gather(norm_back(inv_four, normed_four, own_cot * gain_four).astype(bf16)), axis=0
    )
    grad_hidden = times_rows(grad_ffn, down_all)
    grad_gate = gelu_pull(grad_hidden * up_lin)[0].astype(bf16)
    grad_up = (grad_hidden * activated).astype(bf16)
    grad_ffn_in = layer_scatter(
        jnp.concatenate(
            [
                contract(grad_gate, gate_block, 1, 1) + contract(grad_up, up_block, 1, 1)
                for gate_block, up_block in zip(gate_all, up_all)
            ],
            axis=1,
        ).astype(bf16)
    )
    grad_w_down = collect_far(collect_near(weight_parts(grad_ffn, hidden_b)))
    grad_w_gate = collect_far(collect_near(weight_parts(ffn_input, grad_gate)))
    grad_w_up = collect_far(collect_near(weight_parts(ffn_input, grad_up)))
    grad_gain_three = jnp.sum(grad_ffn_in * normed_three, axis=0)
    grad_res = own_cot + norm_back(inv_three, normed_three, grad_ffn_in * gain_three)
    grad_gain_two = jnp.sum(grad_res * normed_two, axis=0)

    grad_attn = jnp.concatenate(
        layer_gather(norm_back(inv_two, normed_two, grad_res * gain_two).astype(bf16)), axis=0
    )
    grad_rows = times_rows(grad_attn, out_all).astype(bf16)
    grad_heads = grad_rows.reshape(tok_rows, key_heads, group_size, HD).transpose(1, 2, 0, 3)
    row_delta = jnp.sum(grad_heads.astype(f32) * attn_float, axis=-1)
    probs = jnp.where(visible, jnp.exp(SOFT_CAP * tanh_part - log_total[..., None]), 0.0)
    value_grad = jnp.einsum(
        "jgqc,jgqd->cjd", probs.astype(bf16), grad_heads, preferred_element_type=f32
    )
    weight_grad = jnp.einsum("jgqd,cjd->jgqc", grad_heads, value_h, preferred_element_type=f32)
    score_grad = (
        probs * (weight_grad - row_delta[..., None]) * (1.0 - tanh_part * tanh_part)
    ).astype(bf16)
    grad_q = jnp.einsum("jgqc,cjd->jgqd", score_grad, key_h, preferred_element_type=f32)
    key_grad = jnp.einsum("jgqc,jgqd->cjd", score_grad, queries_h, preferred_element_type=f32)
    pair_grad = jnp.concatenate(
        [key_grad.reshape(key_count, key_width), value_grad.reshape(key_count, key_width)], axis=1
    ).astype(bf16)
    pair_part = collect_near(
        [
            pair_grad[index * 4 * tok_rows : (index + 1) * 4 * tok_rows]
            for index in range(near_count)
        ]
    )
    pair_own = pair_part[:tok_rows].astype(f32)
    for index, step in ((1, far_a), (2, far_b), (3, far_a | far_b)):
        pair_own = pair_own + swap(
            pair_part[index * tok_rows : (index + 1) * tok_rows], step
        ).astype(f32)
    grad_query_lin = (
        rotate(
            grad_q.transpose(2, 0, 1, 3).reshape(tok_rows, heads_local, HD), cos_table, -sine_table
        )
        * HD ** (-0.5)
    ).reshape(tok_rows, query_width)
    grad_key_lin = rotate(
        pair_own[:, :key_width].reshape(tok_rows, key_heads, HD), cos_table, -sine_table
    ).reshape(tok_rows, key_width)
    grad_lin = jnp.concatenate(
        [grad_query_lin, grad_key_lin, pair_own[:, key_width:]], axis=1
    ).astype(bf16)
    grad_attn_in = layer_scatter(times_rows_t(grad_lin, qkv_w).astype(bf16))
    own_inv = rms_scale(own_tok)
    own_normed = own_tok * own_inv
    grad_gain_one = jnp.sum(grad_attn_in * own_normed, axis=0)
    grad_tokens = rows_out(
        layer_gather(
            columns_out(
                grad_res + norm_back(own_inv, own_normed, grad_attn_in * gain_one)
            ).astype(bf16)
        )
    ).astype(f32)

    attn_grads = collect_far(
        collect_near(
            [
                jnp.concatenate([lin_part, out_part], axis=1)
                for lin_part, out_part in zip(
                    weight_parts(attn_input, grad_lin), weight_parts(grad_attn, attn_rows)
                )
            ]
        )
    )
    gain_grads = jnp.stack([grad_gain_one, grad_gain_two, grad_gain_three, grad_gain_four])
    gain_sum = gain_grads
    for bit in [1 << index for index in range(layers.bit_length() - 1)]:
        gain_sum = gain_sum + swap(gain_sum, bit, "tp")
    spread = len(order)
    for bit in reversed([far_a, far_b] + near):
        spread = spread // 2
        gain_sum = gain_sum[:, : spread * shard] + swap(gain_sum[:, spread * shard :], bit)
    return (
        output,
        grad_tokens,
        attn_grads[:, :query_width],
        attn_grads[:, query_width : query_width + key_width],
        attn_grads[:, query_width + key_width : qkv_width],
        attn_grads[:, qkv_width:],
        grad_w_gate,
        grad_w_up,
        grad_w_down,
        gain_sum[0],
        gain_sum[1],
        gain_sum[2],
        gain_sum[3],
    )


def solution(mesh):
    return jax.shard_map(
        local,
        mesh=mesh,
        in_specs=(
            P("ctx", None),
            P("ctx", "tp"),
            P("ctx", "tp"),
            P("ctx", "tp"),
            P("ctx", "tp"),
            P("ctx", "tp"),
            P("ctx", "tp"),
            P("ctx", "tp"),
            P("ctx"),
            P("ctx"),
            P("ctx"),
            P("ctx"),
            P("ctx", None),
        ),
        out_specs=(
            P("ctx", None),
            P("ctx", None),
            P("ctx", "tp"),
            P("ctx", "tp"),
            P("ctx", "tp"),
            P("ctx", "tp"),
            P("ctx", "tp"),
            P("ctx", "tp"),
            P("ctx", "tp"),
            P("ctx"),
            P("ctx"),
            P("ctx"),
            P("ctx"),
        ),
        check_vma=False,
    )
```

```python
import math

import jax
import jax.numpy as jnp
from jax import lax
from jax.sharding import PartitionSpec as P

HD = 256


EPSILON = 1e-06
SOFT_CAP = 50.0
MASKED = -1e30


def rms_scale(values):
    return lax.rsqrt(jnp.mean(values * values, axis=-1, keepdims=True) + EPSILON)


def norm_back(inv_rms, normed, gradient):
    return inv_rms * (gradient - normed * jnp.mean(gradient * normed, axis=-1, keepdims=True))


def rotate(values, cos_table, sine_table):
    half_width = values.shape[-1] // 2
    leading = values[..., :half_width]
    trailing = values[..., half_width:]
    return jnp.concatenate(
        [leading * cos_table - trailing * sine_table, trailing * cos_table + leading * sine_table],
        axis=-1,
    )


def gelu_tanh(values):
    return jax.nn.gelu(values, approximate=True)


def product(first_operand, second_operand):
    return jnp.dot(first_operand, second_operand, preferred_element_type=jnp.float32)


def contract(first_operand, second_operand, first_dim, second_dim):
    return lax.dot_general(
        first_operand,
        second_operand,
        (((first_dim,), (second_dim,)), ((), ())),
        preferred_element_type=jnp.float32,
    )


def after(value, *earlier):
    return lax.optimization_barrier((value,) + earlier)[0]


def local(
    tokens,
    w_query,
    w_key,
    w_value,
    w_out,
    w_gate,
    w_up,
    w_down,
    norm_attn_in,
    norm_attn_out,
    norm_ffn_in,
    norm_ffn_out,
    cotangent,
):
    bf16, f32 = jnp.bfloat16, jnp.float32
    tok_rows, width = tokens.shape
    heads_local = w_query.shape[1] // HD
    key_heads = w_key.shape[1] // HD
    group_size = heads_local // key_heads
    query_width = heads_local * HD
    key_width = key_heads * HD
    ring = lax.axis_size("ctx")
    layers = lax.axis_size("tp")
    me = lax.axis_index("ctx")
    my_layer = lax.axis_index("tp")
    shard = width // ring
    own_rows = tok_rows // layers
    upper = shard // 32 * 16
    far_a, far_b = ring // 4, ring // 2
    near = [1 << bit for bit in range(far_a.bit_length() - 1)]
    order = [0, far_a, far_b, far_a | far_b]
    for bit in near:
        order = order + [block | bit for block in order]
    near_count = ring // 4
    near_width = 4 * shard
    spans = []
    for start in range(0, ring, 4):
        own, for_a, for_b, for_ab = order[start : start + 4]
        spans += [(own, 0), (own, 1), (for_b, 0), (for_a, 1)]
        spans += [(for_a, 0), (for_ab, 0), (for_ab, 1), (for_b, 1)]
    sizes = [shard - upper if half else upper for _, half in spans]
    starts = [sum(sizes[:index]) for index in range(len(sizes))]

    def swap(value, bit, axis="ctx"):
        count = lax.axis_size(axis)
        return lax.ppermute(value, axis, [(index, index ^ bit) for index in range(count)])

    def send_far(piece):
        return swap(piece, far_a), swap(piece, far_b)

    def relay(from_a, from_b):
        return swap(from_b[:upper], far_a), swap(from_a[upper:shard], far_b)

    def far_block(piece, direct, diagonal):
        (a_top, a_bottom), (b_top, b_bottom) = (
            (held[:upper], held[upper:shard]) for held in direct
        )
        return jnp.concatenate(
            [piece[:shard], b_top, a_bottom, a_top, diagonal[0], diagonal[1], b_bottom], axis=0
        )

    def spread_near(block):
        blocks = [block]
        for bit in near:
            blocks = blocks + [swap(held, bit) for held in blocks]
        return blocks

    def reduce_begin(activation, gradient):
        groups = by_near(activation)
        sent = [contract(part, gradient, 0, 0).astype(bf16) for part in groups[near_count // 2 :]]
        return groups[: max(near_count // 2, 1)], gradient, sent if near else []

    def reduce_near(state, *earlier):
        groups, gradient, sent = state
        if earlier:
            gradient = after(gradient, *earlier)
        bounds = (0, 2 * shard, 2 * shard + 2 * upper, 4 * shard)
        arrived = [swap(piece, near[-1]) for piece in sent]
        sums = []
        for index, group in enumerate(groups):
            parts = []
            for low, high in zip(bounds[:-1], bounds[1:]):
                part = contract(group[:, low:high], gradient, 0, 0)
                if arrived:
                    part = part + arrived[index][low:high].astype(f32)
                parts.append(part.astype(bf16))
            sums.append(parts)
        for bit in reversed(near[:-1]):
            half = len(sums) // 2
            sums = [
                [
                    (mine.astype(f32) + swap(piece, bit).astype(f32)).astype(bf16)
                    for mine, piece in zip(kept, sent)
                ]
                for kept, sent in zip(sums[:half], sums[half:])
            ]
        return sums[0]

    def reduce_far(sums, *earlier):
        kept, for_a, for_b = sums
        from_a, from_b = swap(for_a, far_a), swap(for_b, far_b)
        kept_then = after(kept, *earlier) if earlier else kept
        lower = shard - upper
        for_b = kept_then[shard : shard + upper].astype(f32) + from_a[upper:].astype(f32)
        for_a = kept_then[shard + upper :].astype(f32) + from_b[:lower].astype(f32)
        return kept, from_a, from_b, (for_b.astype(bf16), for_a.astype(bf16))

    def reduce_end(state, *columns):
        kept, from_a, from_b, last = state
        last = swap(last[0], far_b), swap(last[1], far_a)
        results = []
        for start, stop in columns:
            own, one, other, top, bottom = (
                piece[:, start:stop].astype(f32) for piece in (kept, from_a, from_b, *last)
            )
            results.append(
                jnp.concatenate(
                    [
                        own[:upper] + one[:upper] + top,
                        own[upper:shard] + other[shard - upper :] + bottom,
                    ],
                    axis=0,
                )
            )
        return results

    def layer_scatter(partial, *earlier):
        pieces = [
            partial[step * own_rows : (step + 1) * own_rows] for step in range(layers)
        ]
        if layers == 4:
            passed_on = swap(pieces[3], 1, "tp")
            arrived = [swap(pieces[1], 1, "tp")]
            pair_sum = (pieces[2].astype(f32) + passed_on.astype(f32)).astype(bf16)
            arrived.append(swap(pair_sum, 2, "tp"))
        else:
            arrived = [swap(pieces[step], step, "tp") for step in range(1, layers)]
        total = after(pieces[0], *earlier) if earlier else pieces[0]
        total = total.astype(f32)
        for piece in arrived:
            total = total + piece.astype(f32)
        return total

    def layer_gather(rows):
        if layers == 4:
            second = swap(rows, 2, "tp")
            first = swap(rows, 1, "tp")
            return [rows, first, second, swap(second, 1, "tp")]
        return [rows] + [swap(rows, step, "tp") for step in range(1, layers)]

    def rows_in(array):
        return jnp.concatenate(
            [
                lax.dynamic_slice_in_dim(array, (my_layer ^ step) * own_rows, own_rows, 0)
                for step in range(layers)
            ],
            axis=0,
        )

    def columns_in(array):
        return jnp.concatenate(
            [
                lax.dynamic_slice_in_dim(array, (me ^ block) * shard + half * upper, size, 1)
                for (block, half), size in zip(spans, sizes)
            ],
            axis=1,
        )

    def columns_out(array):
        def place(block, half):
            in_a, in_b = (block & far_a) // far_a, (block & far_b) // far_b
            values = [
                starts[spans.index((held, half))] for held in (0, far_a, far_b, far_a | far_b)
            ]
            found = (
                values[0]
                + (values[1] - values[0]) * in_a
                + (values[2] - values[0]) * in_b
                + (values[3] + values[0] - values[1] - values[2]) * in_a * in_b
            )
            for index, bit in enumerate(near):
                found = found + (near_width << index) * ((block & bit) // bit)
            return found

        return jnp.concatenate(
            [
                lax.dynamic_slice_in_dim(
                    array, place(me ^ block, half), shard - upper if half else upper, 1
                )
                for block in range(ring)
                for half in (0, 1)
            ],
            axis=1,
        )

    def rows_out(pieces):
        result = jnp.zeros((tok_rows,) + pieces[0].shape[1:], pieces[0].dtype)
        for step, piece in enumerate(pieces):
            result = lax.dynamic_update_slice_in_dim(
                result, piece, (my_layer ^ step) * own_rows, 0
            )
        return result

    def by_near(array):
        return [
            array[:, index * near_width : (index + 1) * near_width] for index in range(near_count)
        ]

    def times_rows(activation, blocks):
        total = None
        for part, block in zip(by_near(activation), blocks):
            term = product(part, block)
            total = term if total is None else total + term
        return total

    def times_rows_t(activation, blocks):
        return jnp.concatenate([contract(activation, block, 1, 1) for block in blocks], axis=1)

    qkv_width = query_width + 2 * key_width
    attn_width = qkv_width + query_width
    first_gain = norm_attn_in.astype(f32)[:, None]
    gain_rows = (
        jnp.zeros((16, attn_width), bf16)
        .at[:3, :shard]
        .set(jnp.stack([norm_attn_out, norm_ffn_in, norm_ffn_out]))
    )
    attn_rows_own = jnp.concatenate(
        [
            (jnp.concatenate([w_query, w_key, w_value], axis=1).astype(f32) * first_gain).astype(
                bf16
            ),
            w_out,
        ],
        axis=1,
    )
    gate_up = lax.all_gather(
        jnp.concatenate([w_gate, w_up], axis=1), "ctx", axis=0, tiled=True
    )
    down_w = lax.all_gather(w_down, "ctx", axis=0, tiled=True)
    attn_direct = send_far(jnp.concatenate([attn_rows_own, gain_rows], axis=0))
    attn_diagonal = relay(*attn_direct)
    attn_w = spread_near(far_block(attn_rows_own, attn_direct, attn_diagonal))
    qkv_w = [block[:, :qkv_width] for block in attn_w]
    out_w = [block[:, qkv_width:] for block in attn_w]
    own_gains = jnp.stack([norm_attn_out, norm_ffn_in, norm_ffn_out])
    gain_a, gain_b = (held[shard : shard + 3, :shard] for held in attn_direct)
    gains_far = jnp.concatenate(
        [
            own_gains,
            gain_b[:, :upper],
            gain_a[:, upper:],
            gain_a[:, :upper],
            swap(gain_b, far_a),
            gain_b[:, upper:],
        ],
        axis=1,
    )
    gain_two, gain_three, gain_four = jnp.split(
        columns_out(jnp.concatenate(spread_near(gains_far), axis=1)).astype(f32), 3
    )

    tok_float = rows_in(tokens).astype(f32)
    own_cot = lax.dynamic_slice_in_dim(cotangent, my_layer * own_rows, own_rows, 0).astype(f32)
    attn_input = columns_in((tok_float * rms_scale(tok_float)).astype(bf16))
    own_tok = tok_float[:own_rows]
    lin = times_rows(attn_input, qkv_w)
    row_place = jnp.concatenate(
        [
            (my_layer ^ step) * own_rows + jnp.arange(own_rows, dtype=jnp.int32)
            for step in range(layers)
        ]
    )
    query_pos = me * tok_rows + row_place
    half_width = HD // 2
    frequency = jnp.exp(
        jnp.arange(half_width, dtype=f32) * (-2.0 * math.log(10000.0) / HD)
    )
    angles = query_pos.astype(f32)[:, None] * frequency[None, :]
    cos_table, sine_table = jnp.cos(angles)[:, None, :], jnp.sin(angles)[:, None, :]
    queries = (
        rotate(lin[:, :query_width].reshape(tok_rows, heads_local, HD), cos_table, sine_table)
        * HD ** (-0.5)
    ).astype(bf16)
    queries_h = queries.reshape(tok_rows, key_heads, group_size, HD).transpose(1, 2, 0, 3)
    keys_rot = (
        rotate(
            lin[:, query_width : query_width + key_width].reshape(tok_rows, key_heads, HD),
            cos_table,
            sine_table,
        )
        .astype(bf16)
        .reshape(tok_rows, key_width)
    )
    values_b = lin[:, query_width + key_width :].astype(bf16)
    pair = jnp.concatenate([keys_rot, values_b], axis=1)
    pair_steps = [swap(pair, step) for step in (far_a, far_b, far_a | far_b)]
    pair_far = jnp.concatenate([pair] + pair_steps, axis=0)
    pairs = jnp.concatenate(spread_near(pair_far), axis=0)
    key_count = pairs.shape[0]
    key_h = pairs[:, :key_width].reshape(key_count, key_heads, HD)
    value_h = pairs[:, key_width:].reshape(key_count, key_heads, HD)
    key_pos = jnp.concatenate([(me ^ block) * tok_rows + row_place for block in order])
    visible = key_pos[None, :] <= query_pos[:, None]
    tanh_part = jnp.tanh(
        jnp.einsum("jgqd,cjd->jgqc", queries_h, key_h, preferred_element_type=f32) / SOFT_CAP
    )
    capped = jnp.where(visible, SOFT_CAP * tanh_part, MASKED)
    row_max = jnp.max(capped, axis=-1)
    weights = jnp.where(visible, jnp.exp(capped - row_max[..., None]), 0.0)
    row_sum = jnp.sum(weights, axis=-1)
    attn_float = (
        jnp.einsum("jgqc,cjd->jgqd", weights.astype(bf16), value_h, preferred_element_type=f32)
        / row_sum[..., None]
    )
    log_total = row_max + jnp.log(row_sum)
    attn_rows = attn_float.transpose(2, 0, 1, 3).reshape(tok_rows, query_width).astype(bf16)
    attn_part = times_rows_t(attn_rows, out_w).astype(bf16)
    attn_total = columns_out(layer_scatter(attn_part))
    inv_two = rms_scale(attn_total)
    normed_two = attn_total * inv_two
    hidden_res = own_tok + normed_two * gain_two
    inv_three = rms_scale(hidden_res)
    normed_three = hidden_res * inv_three
    ffn_input = jnp.concatenate(layer_gather((normed_three * gain_three).astype(bf16)), axis=0)

    ffn_width = w_gate.shape[1]
    both_lin = product(ffn_input, gate_up)
    gate_lin, up_lin = both_lin[:, :ffn_width], both_lin[:, ffn_width:]
    activated, gelu_pull = jax.vjp(gelu_tanh, gate_lin)
    hidden_b = (activated * up_lin).astype(bf16)
    ffn_total = layer_scatter(contract(hidden_b, down_w, 1, 1).astype(bf16))
    inv_four = rms_scale(ffn_total)
    normed_four = ffn_total * inv_four
    own_output = (hidden_res + normed_four * gain_four).astype(bf16)
    grad_gain_four = jnp.sum(own_cot * normed_four, axis=0)
    grad_ffn = jnp.concatenate(
        layer_gather(norm_back(inv_four, normed_four, own_cot * gain_four).astype(bf16)), axis=0
    )
    down_sum = lax.psum_scatter(
        contract(grad_ffn, hidden_b, 0, 0).astype(bf16), "ctx", scatter_dimension=0, tiled=True
    )
    grad_hidden = product(grad_ffn, down_w)
    grad_gate = gelu_pull(grad_hidden * up_lin)[0].astype(bf16)
    grad_up = (grad_hidden * activated).astype(bf16)
    grad_both = jnp.concatenate([grad_gate, grad_up], axis=1)
    grad_in_part = contract(grad_both, gate_up, 1, 1).astype(bf16)
    grad_ffn_in = layer_scatter(grad_in_part)
    both_sum = lax.psum_scatter(
        contract(ffn_input, after(grad_both, grad_in_part), 0, 0).astype(bf16),
        "ctx",
        scatter_dimension=0,
        tiled=True,
    )
    grad_gain_three = jnp.sum(grad_ffn_in * normed_three, axis=0)
    grad_res = own_cot + norm_back(inv_three, normed_three, grad_ffn_in * gain_three)
    grad_gain_two = jnp.sum(grad_res * normed_two, axis=0)

    grad_attn = jnp.concatenate(
        layer_gather(columns_in(norm_back(inv_two, normed_two, grad_res * gain_two).astype(bf16))),
        axis=0,
    )
    grad_rows = times_rows(grad_attn, out_w).astype(bf16)
    grad_heads = grad_rows.reshape(tok_rows, key_heads, group_size, HD).transpose(1, 2, 0, 3)
    row_delta = jnp.sum(grad_heads.astype(f32) * attn_float, axis=-1)
    probs = jnp.where(visible, jnp.exp(SOFT_CAP * tanh_part - log_total[..., None]), 0.0)
    value_grad = jnp.einsum(
        "jgqc,jgqd->cjd", probs.astype(bf16), grad_heads, preferred_element_type=f32
    )
    weight_grad = jnp.einsum("jgqd,cjd->jgqc", grad_heads, value_h, preferred_element_type=f32)
    score_grad = (
        probs * (weight_grad - row_delta[..., None]) * (1.0 - tanh_part * tanh_part)
    ).astype(bf16)
    grad_q = jnp.einsum("jgqc,cjd->jgqd", score_grad, key_h, preferred_element_type=f32)
    key_grad = jnp.einsum("jgqc,jgqd->cjd", score_grad, queries_h, preferred_element_type=f32)
    pair_grad = jnp.concatenate(
        [key_grad.reshape(key_count, key_width), value_grad.reshape(key_count, key_width)], axis=1
    ).astype(bf16)
    pair_part = [
        pair_grad[index * 4 * tok_rows : (index + 1) * 4 * tok_rows] for index in range(near_count)
    ]
    for bit in reversed(near):
        half = len(pair_part) // 2
        pair_part = [
            (kept.astype(f32) + swap(sent, bit).astype(f32)).astype(bf16)
            for kept, sent in zip(pair_part[:half], pair_part[half:])
        ]
    pair_part = pair_part[0]
    output = rows_out(layer_gather(after(own_output, pair_part)))
    out_sums = reduce_near(reduce_begin(after(grad_attn, pair_part), attn_rows))
    pair_own = pair_part[:tok_rows].astype(f32)
    for index, step in ((1, far_a), (2, far_b), (3, far_a | far_b)):
        pair_own = pair_own + swap(
            pair_part[index * tok_rows : (index + 1) * tok_rows], step
        ).astype(f32)
    pair_own = after(pair_own, *out_sums)
    grad_query_lin = (
        rotate(
            grad_q.transpose(2, 0, 1, 3).reshape(tok_rows, heads_local, HD), cos_table, -sine_table
        )
        * HD ** (-0.5)
    ).reshape(tok_rows, query_width)
    grad_key_lin = rotate(
        pair_own[:, :key_width].reshape(tok_rows, key_heads, HD), cos_table, -sine_table
    ).reshape(tok_rows, key_width)
    grad_lin = jnp.concatenate(
        [grad_query_lin, grad_key_lin, pair_own[:, key_width:]], axis=1
    ).astype(bf16)
    grad_in_part = times_rows_t(grad_lin, qkv_w).astype(bf16)
    lin_sums = reduce_near(reduce_begin(after(attn_input, grad_in_part), grad_lin))
    grad_attn_in = columns_out(layer_scatter(grad_in_part, *lin_sums, *out_sums))
    lin_far = reduce_far(lin_sums)
    out_far = reduce_far(out_sums)
    own_inv = rms_scale(own_tok)
    own_normed = own_tok * own_inv
    grad_gain_one = jnp.sum(grad_attn_in * own_normed, axis=0)
    token_pieces = layer_gather(
        (grad_res + norm_back(own_inv, own_normed, grad_attn_in)).astype(bf16)
    )
    grad_tokens = rows_out(token_pieces).astype(f32)

    grad_w_query, grad_w_key, grad_w_value = reduce_end(
        lin_far,
        (0, query_width),
        (query_width, query_width + key_width),
        (query_width + key_width, qkv_width),
    )
    (grad_w_out,) = reduce_end(out_far, (0, query_width))
    gain_grads = columns_in(
        jnp.stack([grad_gain_one, grad_gain_two, grad_gain_three, grad_gain_four])
    )
    gain_sum = after(gain_grads, token_pieces[2])
    for bit in [1 << index for index in range(layers.bit_length() - 1)]:
        gain_sum = gain_sum + swap(gain_sum, bit, "tp")
    for bit in reversed(near):
        half = gain_sum.shape[1] // 2
        gain_sum = gain_sum[:, :half] + swap(gain_sum[:, half:], bit)
    lower = shard - upper
    from_a = swap(gain_sum[:, 2 * shard : 2 * shard + 2 * upper], far_a)
    from_b = swap(gain_sum[:, 2 * shard + 2 * upper :], far_b)
    last_b = swap(gain_sum[:, shard : shard + upper] + from_a[:, upper:], far_b)
    last_a = swap(gain_sum[:, shard + upper : 2 * shard] + from_b[:, :lower], far_a)
    gain_sum = jnp.concatenate(
        [
            gain_sum[:, :upper] + from_a[:, :upper] + last_b,
            gain_sum[:, upper:shard] + from_b[:, lower:] + last_a,
        ],
        axis=1,
    )
    return (
        output,
        grad_tokens,
        grad_w_query * first_gain,
        grad_w_key * first_gain,
        grad_w_value * first_gain,
        grad_w_out,
        both_sum[:, :ffn_width].astype(f32),
        both_sum[:, ffn_width:].astype(f32),
        down_sum.astype(f32),
        gain_sum[0] / first_gain[:, 0],
        gain_sum[1],
        gain_sum[2],
        gain_sum[3],
    )


def solution(mesh):
    return jax.shard_map(
        local,
        mesh=mesh,
        in_specs=(
            P("ctx", None),
            P("ctx", "tp"),
            P("ctx", "tp"),
            P("ctx", "tp"),
            P("ctx", "tp"),
            P("ctx", "tp"),
            P("ctx", "tp"),
            P("ctx", "tp"),
            P("ctx"),
            P("ctx"),
            P("ctx"),
            P("ctx"),
            P("ctx", None),
        ),
        out_specs=(
            P("ctx", None),
            P("ctx", None),
            P("ctx", "tp"),
            P("ctx", "tp"),
            P("ctx", "tp"),
            P("ctx", "tp"),
            P("ctx", "tp"),
            P("ctx", "tp"),
            P("ctx", "tp"),
            P("ctx"),
            P("ctx"),
            P("ctx"),
            P("ctx"),
        ),
        check_vma=False,
    )
```

```python
import functools
import math

import jax
import jax.numpy as jnp
from jax import lax
from jax.experimental import pallas as pl
from jax.experimental.pallas import tpu as pltpu
from jax.sharding import PartitionSpec as P

HD = 256


EPSILON = 1e-06
SOFT_CAP = 50.0
MASKED = -1e30

bf16, f32 = jnp.bfloat16, jnp.float32


def rms_scale(values):
    return lax.rsqrt(jnp.mean(values * values, axis=-1, keepdims=True) + EPSILON)


def norm_back(inv_rms, normed, gradient):
    return inv_rms * (gradient - normed * jnp.mean(gradient * normed, axis=-1, keepdims=True))


def rotate(values, cos_table, sine_table):
    half_width = values.shape[-1] // 2
    leading = values[..., :half_width]
    trailing = values[..., half_width:]
    return jnp.concatenate(
        [leading * cos_table - trailing * sine_table, trailing * cos_table + leading * sine_table],
        axis=-1,
    )


def gelu_tanh(values):
    return jax.nn.gelu(values, approximate=True)


def product(first_operand, second_operand):
    return jnp.dot(first_operand, second_operand, preferred_element_type=f32)


def contract(first_operand, second_operand, first_dim, second_dim):
    return lax.dot_general(
        first_operand,
        second_operand,
        (((first_dim,), (second_dim,)), ((), ())),
        preferred_element_type=f32,
    )


def after(value, *earlier):
    return lax.optimization_barrier((value,) + earlier)[0]


def swap(value, bit, axis="ctx"):
    count = lax.axis_size(axis)
    return lax.ppermute(value, axis, [(index, index ^ bit) for index in range(count)])


WHOLE = pl.BlockSpec(memory_space=pltpu.VMEM)
SCALARS = pl.BlockSpec(memory_space=pltpu.SMEM)
VMEM_BYTES = 24 * 2**20


def shape_of(dims, kind):
    return jax.ShapeDtypeStruct(dims, kind)


def key_block(key_count):
    return math.gcd(key_count, 512)


def attend_kernel(steps, group, query_ref, pair_ref, place_ref, key_place_ref, out_ref, rows_ref, log_ref):
    step = pl.program_id(0)
    rows = place_ref.shape[0]

    @pl.when(step == 0)
    def _():
        out_ref[...] = jnp.zeros_like(out_ref)
        log_ref[...] = jnp.zeros_like(log_ref)

    keys, values = pair_ref[:, :HD], pair_ref[:, HD:]
    scores = contract(query_ref[...], keys, 1, 1)
    capped = SOFT_CAP * jnp.tanh(scores * (1.0 / SOFT_CAP))
    visible = key_place_ref[...] <= place_ref[...]
    weights = jnp.where(visible, jnp.exp(capped), 0.0)
    log_ref[...] += jnp.sum(weights, axis=-1, keepdims=True)
    out_ref[...] += product(weights.astype(bf16), values)

    @pl.when(step == steps - 1)
    def _():
        total = log_ref[...]
        result = out_ref[...] / total
        out_ref[...] = result
        log_ref[...] = jnp.log(total)
        each = rows // group
        for head in range(group):
            rows_ref[:, head * HD : (head + 1) * HD] = result[head * each : (head + 1) * each].astype(bf16)


def attend(queries, pairs, places, key_places, group):
    rows, key_count = queries.shape[0], pairs.shape[0]
    block = key_block(key_count)
    steps = key_count // block
    fixed = lambda step: (0, 0)
    return pl.pallas_call(
        functools.partial(attend_kernel, steps, group),
        grid=(steps,),
        in_specs=[
            pl.BlockSpec((rows, HD), fixed),
            pl.BlockSpec((block, 2 * HD), lambda step: (step, 0)),
            pl.BlockSpec((rows, 1), fixed),
            pl.BlockSpec((1, block), lambda step: (0, step)),
        ],
        out_specs=[
            pl.BlockSpec((rows, HD), fixed),
            pl.BlockSpec((rows // group, group * HD), fixed),
            pl.BlockSpec((rows, 1), fixed),
        ],
        out_shape=[
            shape_of((rows, HD), f32),
            shape_of((rows // group, group * HD), bf16),
            shape_of((rows, 1), f32),
        ],
        compiler_params=pltpu.CompilerParams(vmem_limit_bytes=VMEM_BYTES),
        name="attend",
    )(queries, pairs, places, key_places)


def attend_back_kernel(
    query_ref, grad_ref, out_ref, log_ref, pair_ref, place_ref, key_place_ref, query_grad_ref, pair_grad_ref, delta_ref
):
    @pl.when(pl.program_id(0) == 0)
    def _():
        query_grad_ref[...] = jnp.zeros_like(query_grad_ref)
        delta_ref[...] = jnp.sum(grad_ref[...].astype(f32) * out_ref[...], axis=-1, keepdims=True)

    queries, grads = query_ref[...], grad_ref[...]
    keys, values = pair_ref[:, :HD], pair_ref[:, HD:]
    part = jnp.tanh(contract(queries, keys, 1, 1) * (1.0 / SOFT_CAP))
    visible = key_place_ref[...] <= place_ref[...]
    probs = jnp.where(visible, jnp.exp(SOFT_CAP * part - log_ref[...]), 0.0)
    pair_grad_ref[:, HD:] = contract(probs.astype(bf16), grads, 0, 0).astype(bf16)
    slope = contract(grads, values, 1, 1) - delta_ref[...]
    score_grad = (probs * slope * (1.0 - part * part)).astype(bf16)
    query_grad_ref[...] += product(score_grad, keys)
    pair_grad_ref[:, :HD] = contract(score_grad, queries, 0, 0).astype(bf16)


def attend_back(queries, grads, outs, logs, pairs, places, key_places):
    rows, key_count = queries.shape[0], pairs.shape[0]
    block = key_block(key_count)
    fixed = lambda step: (0, 0)
    tall = pl.BlockSpec((rows, HD), fixed)
    column = pl.BlockSpec((rows, 1), fixed)
    moving = pl.BlockSpec((block, 2 * HD), lambda step: (step, 0))
    return pl.pallas_call(
        attend_back_kernel,
        grid=(key_count // block,),
        in_specs=[tall, tall, tall, column, moving, column, pl.BlockSpec((1, block), lambda step: (0, step))],
        out_specs=[tall, moving],
        out_shape=[shape_of((rows, HD), f32), shape_of((key_count, 2 * HD), bf16)],
        scratch_shapes=[pltpu.VMEM((rows, 1), f32)],
        compiler_params=pltpu.CompilerParams(vmem_limit_bytes=VMEM_BYTES),
        name="attend_back",
    )(queries, grads, outs, logs, pairs, places, key_places)


def local(
    tokens,
    w_query,
    w_key,
    w_value,
    w_out,
    w_gate,
    w_up,
    w_down,
    norm_attn_in,
    norm_attn_out,
    norm_ffn_in,
    norm_ffn_out,
    cotangent,
):
    tok_rows, width = tokens.shape
    heads_local = w_query.shape[1] // HD
    key_heads = w_key.shape[1] // HD
    query_width = heads_local * HD
    key_width = key_heads * HD
    qkv_width = query_width + 2 * key_width
    ffn_width = w_gate.shape[1]
    ring = lax.axis_size("ctx")
    layers = lax.axis_size("tp")
    me = lax.axis_index("ctx")
    my_layer = lax.axis_index("tp")
    shard = width // ring
    own_rows = tok_rows // layers
    upper = shard // 32 * 16
    far_a, far_b = ring // 4, ring // 2
    near = [1 << bit for bit in range(far_a.bit_length() - 1)]
    order = [0, far_a, far_b, far_a | far_b]
    for bit in near:
        order = order + [block | bit for block in order]
    near_width = 4 * shard
    gather_factors = tok_rows * ring <= width

    def spread_far(piece):
        from_a, from_b = swap(piece, far_a), swap(piece, far_b)
        return from_a, from_b, swap(from_b[:upper], far_a), swap(from_a[upper:shard], far_b)

    def spread_near(block):
        blocks = [block]
        for bit in near:
            blocks = blocks + [swap(held, bit) for held in blocks]
        return blocks

    def by_near(array):
        return [array[:, start : start + near_width] for start in range(0, width, near_width)]

    def times_rows(activation, blocks):
        total = None
        for part, block in zip(by_near(activation), blocks):
            term = product(part, block)
            total = term if total is None else total + term
        return total

    def times_rows_t(activation, blocks):
        return jnp.concatenate([contract(activation, block, 1, 1) for block in blocks], axis=1)

    def layer_scatter(partial, first=None, second=None):
        pieces = [partial[step * own_rows : (step + 1) * own_rows] for step in range(layers)]
        done_first = first(partial) if first else ()
        if layers == 4:
            passed_on = swap(pieces[3], 1, "tp")
            arrived = [swap(pieces[1], 1, "tp")]
            held = after(pieces[2], *done_first) if first else pieces[2]
            pair_sum = (held.astype(f32) + passed_on.astype(f32)).astype(bf16)
            arrived.append(swap(pair_sum, 2, "tp"))
        else:
            pair_sum = partial
            arrived = [swap(pieces[step], step, "tp") for step in range(1, layers)]
        done_second = second(pair_sum) if second else ()
        total = after(pieces[0], *done_first, *done_second).astype(f32)
        for piece in arrived:
            total = total + piece.astype(f32)
        return total, done_first, done_second

    def layer_gather(rows, first=None, second=None):
        done_first = first(rows) if first else ()
        if layers == 4:
            across = swap(rows, 2, "tp")
            beside = swap(rows, 1, "tp")
            across_then = after(across, *done_first) if first else across
            pieces = [rows, beside, across, swap(across_then, 1, "tp")]
        else:
            across_then = rows
            pieces = [rows] + [swap(rows, step, "tp") for step in range(1, layers)]
        done_second = second(across_then) if second else ()
        if first or second:
            pieces[0] = after(pieces[0], *done_first, *done_second)
        return pieces, done_first, done_second

    def rows_in(array):
        return jnp.concatenate(
            [
                lax.dynamic_slice_in_dim(array, (my_layer ^ step) * own_rows, own_rows, 0)
                for step in range(layers)
            ],
            axis=0,
        )

    def rows_out(pieces):
        result = jnp.zeros((tok_rows,) + pieces[0].shape[1:], pieces[0].dtype)
        for step, piece in enumerate(pieces):
            result = lax.dynamic_update_slice_in_dim(
                result, piece, (my_layer ^ step) * own_rows, 0
            )
        return result

    def columns_in(array):
        return jnp.concatenate(
            [lax.dynamic_slice_in_dim(array, (me ^ block) * shard, shard, 1) for block in order],
            axis=1,
        )

    def columns_out(array):
        def place(block):
            found = (block & far_a) // far_a + 2 * ((block & far_b) // far_b)
            for index, bit in enumerate(near):
                found = found + (4 << index) * ((block & bit) // bit)
            return found

        return jnp.concatenate(
            [
                lax.dynamic_slice_in_dim(array, place(me ^ block) * shard, shard, 1)
                for block in range(ring)
            ],
            axis=1,
        )

    def rows_of_all(array):
        return lax.all_gather(array, "ctx", axis=0, tiled=True)

    def columns_by_owner(*arrays):
        stacked = jnp.stack([array.reshape(tok_rows, ring, shard) for array in arrays])
        return stacked.transpose(2, 0, 1, 3)

    def columns_of_owner(stacked):
        found = lax.all_to_all(stacked, "ctx", split_axis=0, concat_axis=0, tiled=True)
        return [
            found[:, index].reshape(ring * tok_rows, shard) for index in range(found.shape[1])
        ]

    def sum_scatter(partial):
        return lax.psum_scatter(
            partial.astype(bf16), "ctx", scatter_dimension=0, tiled=True
        ).astype(f32)

    def products_kernel(me_ref, input_ref, lin_ref, grad_ref, rows_ref, out_ref):
        for place, block in enumerate(order):
            rows = pl.ds(pl.multiple_of((me_ref[0] ^ block) * shard, 16), shard)
            here = slice(place * shard, (place + 1) * shard)
            out_ref[rows, :qkv_width] = contract(input_ref[:, here], lin_ref[...], 0, 0).astype(bf16)
            out_ref[rows, qkv_width:] = contract(grad_ref[:, here], rows_ref[...], 0, 0).astype(bf16)

    def attn_products(inputs, lin, grads, rows):
        if shard % 16:
            return jnp.concatenate(
                [
                    contract(columns_out(inputs), lin, 0, 0),
                    contract(columns_out(grads), rows, 0, 0),
                ],
                axis=1,
            ).astype(bf16)
        return pl.pallas_call(
            products_kernel,
            in_specs=[SCALARS] + [WHOLE] * 4,
            out_specs=WHOLE,
            out_shape=shape_of((width, qkv_width + query_width), bf16),
            compiler_params=pltpu.CompilerParams(vmem_limit_bytes=VMEM_BYTES),
            name="attn_products",
        )(me[None], inputs, lin, grads, rows)

    first_gain = norm_attn_in.astype(f32)[:, None]
    gate_up = rows_of_all(jnp.concatenate([w_gate, w_up], axis=1))
    down_w = rows_of_all(w_down)
    qkv_own = (
        jnp.concatenate([w_query, w_key, w_value], axis=1).astype(f32) * first_gain
    ).astype(bf16)
    attn_own = jnp.concatenate([qkv_own, w_out], axis=1)
    own_gains = jnp.stack([norm_attn_out, norm_ffn_in, norm_ffn_out])
    gain_rows = jnp.zeros((16, attn_own.shape[1]), bf16).at[:3, :shard].set(own_gains)
    from_a, from_b, top, bottom = spread_far(jnp.concatenate([attn_own, gain_rows], axis=0))
    attn_w = spread_near(
        jnp.concatenate([attn_own, from_a[:shard], from_b[:shard], top, bottom], axis=0)
    )
    qkv_w = [block[:, :qkv_width] for block in attn_w]
    out_w = [block[:, qkv_width:] for block in attn_w]
    gain_a, gain_b = (held[shard : shard + 3, :shard] for held in (from_a, from_b))
    gains = jnp.concatenate(
        spread_near(
            jnp.concatenate([own_gains, gain_a, gain_b, swap(gain_b, far_a)], axis=1)
        ),
        axis=1,
    )
    gain_two, gain_three, gain_four = jnp.split(columns_out(gains).astype(f32), 3)

    tok_float = rows_in(tokens).astype(f32)
    own_cot = lax.dynamic_slice_in_dim(cotangent, my_layer * own_rows, own_rows, 0).astype(f32)
    norm_input = (tok_float * rms_scale(tok_float)).astype(bf16)
    own_tok = tok_float[:own_rows]
    attn_input = columns_in(norm_input)
    lin = times_rows(attn_input, qkv_w)
    row_place = jnp.concatenate(
        [
            (my_layer ^ step) * own_rows + jnp.arange(own_rows, dtype=jnp.int32)
            for step in range(layers)
        ]
    )
    query_pos = me * tok_rows + row_place
    half_width = HD // 2
    frequency = jnp.exp(jnp.arange(half_width, dtype=f32) * (-2.0 * math.log(10000.0) / HD))
    angles = query_pos.astype(f32)[:, None] * frequency[None, :]
    cos_table, sine_table = jnp.cos(angles)[:, None, :], jnp.sin(angles)[:, None, :]
    queries = (
        rotate(lin[:, :query_width].reshape(tok_rows, heads_local, HD), cos_table, sine_table)
        * HD ** (-0.5)
    ).astype(bf16)
    assert key_heads == 1
    query_rows = queries.reshape(tok_rows, heads_local, HD).transpose(1, 0, 2).reshape(-1, HD)
    keys_rot = (
        rotate(
            lin[:, query_width : query_width + key_width].reshape(tok_rows, key_heads, HD),
            cos_table,
            sine_table,
        )
        .astype(bf16)
        .reshape(tok_rows, key_width)
    )
    values_b = lin[:, query_width + key_width :].astype(bf16)
    pair = jnp.concatenate([keys_rot, values_b], axis=1)
    pair_far = jnp.concatenate(
        [pair] + [swap(pair, step) for step in (far_a, far_b, far_a | far_b)], axis=0
    )
    pairs = jnp.concatenate(spread_near(pair_far), axis=0)
    key_count = pairs.shape[0]
    key_places = jnp.concatenate([(me ^ block) * tok_rows + row_place for block in order])[None, :]
    places = jnp.tile(query_pos, heads_local)[:, None]
    attn_float, attn_rows, attn_log = attend(query_rows, pairs, places, key_places, heads_local)
    attn_total, _, _ = layer_scatter(times_rows_t(attn_rows, out_w).astype(bf16))
    attn_total = columns_out(attn_total)
    inv_two = rms_scale(attn_total)
    normed_two = attn_total * inv_two
    hidden_res = own_tok + normed_two * gain_two
    inv_three = rms_scale(hidden_res)
    normed_three = hidden_res * inv_three
    pieces, _, _ = layer_gather((normed_three * gain_three).astype(bf16))
    ffn_input = jnp.concatenate(pieces, axis=0)

    both_lin = product(ffn_input, gate_up)
    gate_lin, up_lin = both_lin[:, :ffn_width], both_lin[:, ffn_width:]
    activated, gelu_pull = jax.vjp(gelu_tanh, gate_lin)
    hidden_b = (activated * up_lin).astype(bf16)
    if gather_factors:
        all_hidden = rows_of_all(hidden_b)
    ffn_total, _, _ = layer_scatter(contract(hidden_b, down_w, 1, 1).astype(bf16))
    inv_four = rms_scale(ffn_total)
    normed_four = ffn_total * inv_four
    own_output = (hidden_res + normed_four * gain_four).astype(bf16)

    grad_gain_four = jnp.sum(own_cot * normed_four, axis=0)
    pieces, _, _ = layer_gather(norm_back(inv_four, normed_four, own_cot * gain_four).astype(bf16))
    grad_ffn = jnp.concatenate(pieces, axis=0)
    sent_output = after(own_output, grad_ffn)
    if layers == 4:
        output_pieces = [own_output, swap(sent_output, 1, "tp"), swap(sent_output, 2, "tp")]
    else:
        output_pieces, _, _ = layer_gather(sent_output)
    grad_hidden = product(grad_ffn, down_w)
    grad_gate = gelu_pull(grad_hidden * up_lin)[0].astype(bf16)
    grad_up = (grad_hidden * activated).astype(bf16)
    grad_both = jnp.concatenate([grad_gate, grad_up], axis=1)
    if gather_factors:
        all_both = rows_of_all(after(grad_both, all_hidden))
    else:
        grad_w_down = sum_scatter(contract(grad_ffn, hidden_b, 0, 0))
        grad_w_both = sum_scatter(contract(ffn_input, grad_both, 0, 0))
        grad_w_gate, grad_w_up = grad_w_both[:, :ffn_width], grad_w_both[:, ffn_width:]
    grad_in_part = contract(grad_both, gate_up, 1, 1).astype(bf16)
    grad_in_part = after(grad_in_part, *output_pieces[1:])
    if gather_factors:
        grad_ffn_in, (by_owner,), _ = layer_scatter(
            grad_in_part, lambda then: (columns_by_owner(ffn_input, after(grad_ffn, then)),)
        )
    else:
        grad_ffn_in, _, _ = layer_scatter(grad_in_part)
    grad_res = own_cot + norm_back(inv_three, normed_three, grad_ffn_in * gain_three)
    grad_gain_two = jnp.sum(grad_res * normed_two, axis=0)

    own_grad_attn = norm_back(inv_two, normed_two, grad_res * gain_two)
    pieces, _, _ = layer_gather(columns_in(own_grad_attn.astype(bf16)))
    grad_attn = jnp.concatenate(pieces, axis=0)
    grad_rows = times_rows(grad_attn, out_w).astype(bf16)
    grad_heads = grad_rows.reshape(tok_rows, heads_local, HD).transpose(1, 0, 2).reshape(-1, HD)
    grad_q, pair_grad = attend_back(
        query_rows, grad_heads, attn_float, attn_log, pairs, places, key_places
    )
    near_rows = 4 * tok_rows
    pair_part = [
        pair_grad[start : start + near_rows] for start in range(0, key_count, near_rows)
    ]
    for bit in reversed(near):
        half = len(pair_part) // 2
        pair_part = [
            (kept.astype(f32) + swap(sent, bit).astype(f32)).astype(bf16)
            for kept, sent in zip(pair_part[:half], pair_part[half:])
        ]
    pair_part = pair_part[0]
    if layers == 4:
        output_pieces.append(swap(after(output_pieces[2], grad_rows), 1, "tp"))
    output = rows_out(output_pieces)
    arrived = [
        swap(pair_part[index * tok_rows : (index + 1) * tok_rows], step)
        for index, step in ((1, far_a), (2, far_b), (3, far_a | far_b))
    ]
    if gather_factors:
        ffn_cols, down_cols = columns_of_owner(after(by_owner, arrived[0]))
    pair_own = pair_part[:tok_rows].astype(f32)
    for piece in arrived:
        pair_own = pair_own + piece.astype(f32)
    grad_query_lin = (
        rotate(
            grad_q.reshape(heads_local, tok_rows, HD).transpose(1, 0, 2), cos_table, -sine_table
        )
        * HD ** (-0.5)
    ).reshape(tok_rows, query_width)
    grad_key_lin = rotate(
        pair_own[:, :key_width].reshape(tok_rows, key_heads, HD), cos_table, -sine_table
    ).reshape(tok_rows, key_width)
    grad_lin = jnp.concatenate(
        [grad_query_lin, grad_key_lin, pair_own[:, key_width:]], axis=1
    ).astype(bf16)
    grad_in_part = times_rows_t(grad_lin, qkv_w).astype(bf16)

    def products(then):
        lin = after(grad_lin, then, all_both) if gather_factors else after(grad_lin, then)
        return (attn_products(attn_input, lin, grad_attn, attn_rows),)

    def gate_gradient(then):
        return (contract(after(ffn_cols, then), all_both[:, :ffn_width], 0, 0),)

    def up_gradient(then):
        return (contract(after(ffn_cols, then), all_both[:, ffn_width:], 0, 0),)

    def down_gradient(then):
        return (contract(after(down_cols, then), all_hidden, 0, 0),)

    grad_attn_total, (partial,), _ = layer_scatter(grad_in_part, products)
    if gather_factors:
        grad_attn_total = after(grad_attn_total, ffn_cols, down_cols)
    attn_sums = sum_scatter(partial)
    grad_w_lin, grad_w_out = attn_sums[:, :qkv_width], attn_sums[:, qkv_width:]
    grad_attn_in = columns_out(grad_attn_total)
    own_inv = rms_scale(own_tok)
    own_normed = own_tok * own_inv
    own_grad = (grad_res + norm_back(own_inv, own_normed, grad_attn_in)).astype(bf16)
    if gather_factors:
        token_pieces, (grad_w_gate,), _ = layer_gather(own_grad, gate_gradient)
        (grad_w_up,) = up_gradient(token_pieces[3])
        (grad_w_down,) = down_gradient(grad_w_up)
    else:
        token_pieces, _, _ = layer_gather(own_grad)
    grad_tokens = rows_out(token_pieces).astype(f32)

    third_gain = norm_ffn_in.astype(f32)
    gain_third = (
        jnp.sum(w_gate.astype(f32) * grad_w_gate + w_up.astype(f32) * grad_w_up, axis=1)
        / third_gain
    )[None, :]
    gain_sum = columns_in(
        jnp.stack([jnp.sum(grad_attn_in * own_normed, axis=0), grad_gain_two, grad_gain_four])
    )
    gain_sum = after(gain_sum, token_pieces[2])
    for bit in [1 << index for index in range(layers.bit_length() - 1)]:
        gain_third = gain_third + swap(gain_third, bit, "tp")
        gain_sum = gain_sum + swap(gain_sum, bit, "tp")
    for bit in reversed(near):
        half = gain_sum.shape[1] // 2
        gain_sum = gain_sum[:, :half] + swap(gain_sum[:, half:], bit)
    own_gain = gain_sum[:, :shard]
    for index, step in ((1, far_a), (2, far_b), (3, far_a | far_b)):
        own_gain = own_gain + swap(gain_sum[:, index * shard : (index + 1) * shard], step)
    return (
        output,
        grad_tokens,
        grad_w_lin[:, :query_width] * first_gain,
        grad_w_lin[:, query_width : query_width + key_width] * first_gain,
        grad_w_lin[:, query_width + key_width :] * first_gain,
        grad_w_out,
        grad_w_gate,
        grad_w_up,
        grad_w_down,
        own_gain[0] / first_gain[:, 0],
        own_gain[1],
        gain_third[0],
        own_gain[2],
    )


def solution(mesh):
    rows, block = P("ctx", None), P("ctx", "tp")
    gain = P("ctx")
    return jax.shard_map(
        local,
        mesh=mesh,
        in_specs=(rows,) + (block,) * 7 + (gain,) * 4 + (rows,),
        out_specs=(rows, rows) + (block,) * 7 + (gain,) * 4,
        check_vma=False,
    )
```

```python
import functools
import math

import jax
import jax.numpy as jnp
from jax import lax
from jax.experimental import pallas as pl
from jax.experimental.pallas import tpu as pltpu
from jax.sharding import PartitionSpec as P

HD = 256


EPSILON = 1e-06
SOFT_CAP = 50.0
MASKED = -1e30

bf16, f32 = jnp.bfloat16, jnp.float32


def rms_scale(values):
    return lax.rsqrt(jnp.mean(values * values, axis=-1, keepdims=True) + EPSILON)


def norm_back(inv_rms, normed, gradient):
    return inv_rms * (gradient - normed * jnp.mean(gradient * normed, axis=-1, keepdims=True))


def rotate(values, cos_table, sine_table):
    half_width = values.shape[-1] // 2
    leading = values[..., :half_width]
    trailing = values[..., half_width:]
    return jnp.concatenate(
        [leading * cos_table - trailing * sine_table, trailing * cos_table + leading * sine_table],
        axis=-1,
    )


def gelu_tanh(values):
    return jax.nn.gelu(values, approximate=True)


def product(first_operand, second_operand):
    return jnp.dot(first_operand, second_operand, preferred_element_type=f32)


def contract(first_operand, second_operand, first_dim, second_dim):
    return lax.dot_general(
        first_operand,
        second_operand,
        (((first_dim,), (second_dim,)), ((), ())),
        preferred_element_type=f32,
    )


def after(value, *earlier):
    return lax.optimization_barrier((value,) + earlier)[0]


def swap(value, bit, axis="ctx"):
    count = lax.axis_size(axis)
    return lax.ppermute(value, axis, [(index, index ^ bit) for index in range(count)])


WHOLE = pl.BlockSpec(memory_space=pltpu.VMEM)
SCALARS = pl.BlockSpec(memory_space=pltpu.SMEM)
VMEM_BYTES = 24 * 2**20


def shape_of(dims, kind):
    return jax.ShapeDtypeStruct(dims, kind)


def key_block(key_count):
    return math.gcd(key_count, 512)


def attend_kernel(steps, group, query_ref, pair_ref, place_ref, key_place_ref, out_ref, rows_ref, log_ref):
    step = pl.program_id(0)
    rows = place_ref.shape[0]

    @pl.when(step == 0)
    def _():
        out_ref[...] = jnp.zeros_like(out_ref)
        log_ref[...] = jnp.zeros_like(log_ref)

    keys, values = pair_ref[:, :HD], pair_ref[:, HD:]
    scores = contract(query_ref[...], keys, 1, 1)
    capped = SOFT_CAP * jnp.tanh(scores * (1.0 / SOFT_CAP))
    visible = key_place_ref[...] <= place_ref[...]
    weights = jnp.where(visible, jnp.exp(capped), 0.0)
    log_ref[...] += jnp.sum(weights, axis=-1, keepdims=True)
    out_ref[...] += product(weights.astype(bf16), values)

    @pl.when(step == steps - 1)
    def _():
        total = log_ref[...]
        result = out_ref[...] / total
        out_ref[...] = result
        log_ref[...] = jnp.log(total)
        each = rows // group
        for head in range(group):
            rows_ref[:, head * HD : (head + 1) * HD] = result[head * each : (head + 1) * each].astype(bf16)


def attend(queries, pairs, places, key_places, group):
    rows, key_count = queries.shape[0], pairs.shape[0]
    block = key_block(key_count)
    steps = key_count // block
    fixed = lambda step: (0, 0)
    return pl.pallas_call(
        functools.partial(attend_kernel, steps, group),
        grid=(steps,),
        in_specs=[
            pl.BlockSpec((rows, HD), fixed),
            pl.BlockSpec((block, 2 * HD), lambda step: (step, 0)),
            pl.BlockSpec((rows, 1), fixed),
            pl.BlockSpec((1, block), lambda step: (0, step)),
        ],
        out_specs=[
            pl.BlockSpec((rows, HD), fixed),
            pl.BlockSpec((rows // group, group * HD), fixed),
            pl.BlockSpec((rows, 1), fixed),
        ],
        out_shape=[
            shape_of((rows, HD), f32),
            shape_of((rows // group, group * HD), bf16),
            shape_of((rows, 1), f32),
        ],
        compiler_params=pltpu.CompilerParams(vmem_limit_bytes=VMEM_BYTES),
        name="attend",
    )(queries, pairs, places, key_places)


def attend_back_kernel(
    query_ref, grad_ref, out_ref, log_ref, pair_ref, place_ref, key_place_ref, query_grad_ref, pair_grad_ref, delta_ref
):
    @pl.when(pl.program_id(0) == 0)
    def _():
        query_grad_ref[...] = jnp.zeros_like(query_grad_ref)
        delta_ref[...] = jnp.sum(grad_ref[...].astype(f32) * out_ref[...], axis=-1, keepdims=True)

    queries, grads = query_ref[...], grad_ref[...]
    keys, values = pair_ref[:, :HD], pair_ref[:, HD:]
    part = jnp.tanh(contract(queries, keys, 1, 1) * (1.0 / SOFT_CAP))
    visible = key_place_ref[...] <= place_ref[...]
    probs = jnp.where(visible, jnp.exp(SOFT_CAP * part - log_ref[...]), 0.0)
    pair_grad_ref[:, HD:] = contract(probs.astype(bf16), grads, 0, 0).astype(bf16)
    slope = contract(grads, values, 1, 1) - delta_ref[...]
    score_grad = (probs * slope * (1.0 - part * part)).astype(bf16)
    query_grad_ref[...] += product(score_grad, keys)
    pair_grad_ref[:, :HD] = contract(score_grad, queries, 0, 0).astype(bf16)


def attend_back(queries, grads, outs, logs, pairs, places, key_places):
    rows, key_count = queries.shape[0], pairs.shape[0]
    block = key_block(key_count)
    fixed = lambda step: (0, 0)
    tall = pl.BlockSpec((rows, HD), fixed)
    column = pl.BlockSpec((rows, 1), fixed)
    moving = pl.BlockSpec((block, 2 * HD), lambda step: (step, 0))
    return pl.pallas_call(
        attend_back_kernel,
        grid=(key_count // block,),
        in_specs=[tall, tall, tall, column, moving, column, pl.BlockSpec((1, block), lambda step: (0, step))],
        out_specs=[tall, moving],
        out_shape=[shape_of((rows, HD), f32), shape_of((key_count, 2 * HD), bf16)],
        scratch_shapes=[pltpu.VMEM((rows, 1), f32)],
        compiler_params=pltpu.CompilerParams(vmem_limit_bytes=VMEM_BYTES),
        name="attend_back",
    )(queries, grads, outs, logs, pairs, places, key_places)


def local(
    tokens,
    w_query,
    w_key,
    w_value,
    w_out,
    w_gate,
    w_up,
    w_down,
    norm_attn_in,
    norm_attn_out,
    norm_ffn_in,
    norm_ffn_out,
    cotangent,
):
    tok_rows, width = tokens.shape
    heads_local = w_query.shape[1] // HD
    key_heads = w_key.shape[1] // HD
    query_width = heads_local * HD
    key_width = key_heads * HD
    qkv_width = query_width + 2 * key_width
    ffn_width = w_gate.shape[1]
    ring = lax.axis_size("ctx")
    layers = lax.axis_size("tp")
    me = lax.axis_index("ctx")
    my_layer = lax.axis_index("tp")
    shard = width // ring
    own_rows = tok_rows // layers
    upper = shard // 32 * 16
    far_a, far_b = ring // 4, ring // 2
    near = [1 << bit for bit in range(far_a.bit_length() - 1)]
    order = [0, far_a, far_b, far_a | far_b]
    for bit in near:
        order = order + [block | bit for block in order]
    near_width = 4 * shard
    gather_factors = tok_rows * ring <= width

    def spread_far(piece):
        from_a, from_b = swap(piece, far_a), swap(piece, far_b)
        return from_a, from_b, swap(from_b[:upper], far_a), swap(from_a[upper:shard], far_b)

    def spread_near(block):
        blocks = [block]
        for bit in near:
            blocks = blocks + [swap(held, bit) for held in blocks]
        return blocks

    def by_near(array):
        return [array[:, start : start + near_width] for start in range(0, width, near_width)]

    def times_rows(activation, blocks):
        total = None
        for part, block in zip(by_near(activation), blocks):
            term = product(part, block)
            total = term if total is None else total + term
        return total

    def times_rows_t(activation, blocks):
        return jnp.concatenate([contract(activation, block, 1, 1) for block in blocks], axis=1)

    def layer_scatter(partial, first=None, second=None):
        pieces = [partial[step * own_rows : (step + 1) * own_rows] for step in range(layers)]
        done_first = first(partial) if first else ()
        if layers == 4:
            passed_on = swap(pieces[3], 1, "tp")
            arrived = [swap(pieces[1], 1, "tp")]
            held = after(pieces[2], *done_first) if first else pieces[2]
            pair_sum = (held.astype(f32) + passed_on.astype(f32)).astype(bf16)
            arrived.append(swap(pair_sum, 2, "tp"))
        else:
            pair_sum = partial
            arrived = [swap(pieces[step], step, "tp") for step in range(1, layers)]
        done_second = second(pair_sum) if second else ()
        if done_first or done_second:
            arrived[0] = after(arrived[0], *done_first, *done_second)
        return (partial, arrived), done_first, done_second

    def sum_of(parts):
        partial, arrived = parts
        total = partial[:own_rows].astype(f32)
        for piece in arrived:
            total = total + piece.astype(f32)
        return total

    def layer_gather(rows, first=None, second=None):
        done_first = first(rows) if first else ()
        if layers == 4:
            across = swap(rows, 2, "tp")
            beside = swap(rows, 1, "tp")
            across_then = after(across, *done_first) if first else across
            pieces = [rows, beside, across, swap(across_then, 1, "tp")]
        else:
            across_then = rows
            pieces = [rows] + [swap(rows, step, "tp") for step in range(1, layers)]
        done_second = second(across_then) if second else ()
        if first or second:
            pieces[0] = after(pieces[0], *done_first, *done_second)
        return pieces, done_first, done_second

    def rows_in(array):
        return jnp.concatenate(
            [
                lax.dynamic_slice_in_dim(array, (my_layer ^ step) * own_rows, own_rows, 0)
                for step in range(layers)
            ],
            axis=0,
        )

    def rows_out(pieces):
        result = jnp.zeros((tok_rows,) + pieces[0].shape[1:], pieces[0].dtype)
        for step, piece in enumerate(pieces):
            result = lax.dynamic_update_slice_in_dim(
                result, piece, (my_layer ^ step) * own_rows, 0
            )
        return result

    def columns_in(array):
        return jnp.concatenate(
            [lax.dynamic_slice_in_dim(array, (me ^ block) * shard, shard, 1) for block in order],
            axis=1,
        )

    def columns_out(array):
        def place(block):
            found = (block & far_a) // far_a + 2 * ((block & far_b) // far_b)
            for index, bit in enumerate(near):
                found = found + (4 << index) * ((block & bit) // bit)
            return found

        return jnp.concatenate(
            [
                lax.dynamic_slice_in_dim(array, place(me ^ block) * shard, shard, 1)
                for block in range(ring)
            ],
            axis=1,
        )

    def rows_of_all(array):
        return lax.all_gather(array, "ctx", axis=0, tiled=True)

    def in_order(me_ref, source_ref, target_ref, inverse):
        for index in range(ring):

            @pl.when(me_ref[0] == index)
            def _():
                for place, block in enumerate(order):
                    here = slice(place * shard, (place + 1) * shard)
                    there = slice((index ^ block) * shard, ((index ^ block) + 1) * shard)
                    if inverse:
                        target_ref[:, there] = source_ref[:, here]
                    else:
                        target_ref[:, here] = source_ref[:, there]

    in_kernels = ring <= 8 and own_rows % 16 == 0 and layers == 4

    def on_own_rows(body, partial, arrived, others, outs, name, scratch=1):
        def kernel(me_ref, part_ref, one_ref, two_ref, *refs):
            total = part_ref[...].astype(f32) + one_ref[...].astype(f32) + two_ref[...].astype(f32)
            body(me_ref, total, *refs)

        wide = pl.BlockSpec((own_rows, width), lambda step: (0, 0))
        return pl.pallas_call(
            kernel,
            grid=(1,),
            in_specs=[SCALARS, wide] + [WHOLE] * (2 + len(others)),
            out_specs=[WHOLE] * len(outs),
            out_shape=[shape_of((rows, width), kind) for rows, kind in outs],
            scratch_shapes=[pltpu.VMEM((own_rows, width), f32)] * scratch,
            compiler_params=pltpu.CompilerParams(vmem_limit_bytes=VMEM_BYTES),
            name=name,
        )(me[None], partial, *arrived, *others)

    def residual_body(me_ref, total, tok_ref, gain_ref, attn_ref, hidden_ref, input_ref, held_ref):
        held_ref[...] = total
        in_order(me_ref, held_ref, attn_ref, True)
        attn = attn_ref[...]
        hidden = tok_ref[...] + attn * rms_scale(attn) * gain_ref[0:1, :]
        hidden_ref[...] = hidden
        input_ref[...] = (hidden * rms_scale(hidden) * gain_ref[1:2, :]).astype(bf16)

    def output_body(me_ref, total, hidden_ref, cot_ref, gain_ref, out_ref, grad_ref, gain_grad_ref):
        inverse = rms_scale(total)
        normed = total * inverse
        gain, cot = gain_ref[2:3, :], cot_ref[...]
        out_ref[...] = (hidden_ref[...] + normed * gain).astype(bf16)
        gain_grad_ref[...] = jnp.sum(cot * normed, axis=0, keepdims=True)
        grad_ref[...] = norm_back(inverse, normed, cot * gain).astype(bf16)

    def residual_back_body(
        me_ref, total, hidden_ref, attn_ref, cot_ref, gain_ref, res_ref, grad_ref, gain_grad_ref, held_ref, moved_ref
    ):
        hidden, attn = hidden_ref[...], attn_ref[...]
        inverse = rms_scale(hidden)
        res = cot_ref[...] + norm_back(inverse, hidden * inverse, total * gain_ref[1:2, :])
        res_ref[...] = res
        inverse = rms_scale(attn)
        normed = attn * inverse
        gain_grad_ref[...] = jnp.sum(res * normed, axis=0, keepdims=True)
        held_ref[...] = norm_back(inverse, normed, res * gain_ref[0:1, :])
        in_order(me_ref, held_ref, moved_ref, False)
        grad_ref[...] = moved_ref[...].astype(bf16)

    def token_back_body(me_ref, total, tok_ref, res_ref, gain_ref, grad_ref, gain_grad_ref, held_ref, moved_ref):
        held_ref[...] = total
        in_order(me_ref, held_ref, moved_ref, True)
        tok, grad = tok_ref[...], moved_ref[...]
        inverse = rms_scale(tok)
        normed = tok * inverse
        gain_grad_ref[...] = jnp.sum(grad * normed, axis=0, keepdims=True)
        grad_ref[...] = (
            res_ref[...] + norm_back(inverse, normed, grad * gain_ref[3:4, :])
        ).astype(bf16)

    def by_owner_kernel(first_ref, second_ref, out_ref):
        for block in range(ring):
            here = slice(block * shard, (block + 1) * shard)
            out_ref[block, :, :shard] = first_ref[:, here]
            out_ref[block, :, shard:] = second_ref[:, here]

    def columns_by_owner(first, second):
        rows = first.shape[0]
        if not in_kernels:
            stacked = jnp.stack([array.reshape(rows, ring, shard) for array in (first, second)])
            return stacked.transpose(2, 1, 0, 3).reshape(ring, rows, 2 * shard)
        return pl.pallas_call(
            by_owner_kernel,
            in_specs=[WHOLE] * 2,
            out_specs=WHOLE,
            out_shape=shape_of((ring, rows, 2 * shard), bf16),
            compiler_params=pltpu.CompilerParams(vmem_limit_bytes=VMEM_BYTES),
            name="by_owner",
        )(first, second)

    def sum_scatter(partial):
        return lax.psum_scatter(
            partial.astype(bf16), "ctx", scatter_dimension=0, tiled=True
        ).astype(f32)

    def products_kernel(me_ref, input_ref, lin_ref, grad_ref, rows_ref, out_ref):
        for place, block in enumerate(order):
            rows = pl.ds(pl.multiple_of((me_ref[0] ^ block) * shard, 16), shard)
            here = slice(place * shard, (place + 1) * shard)
            out_ref[rows, :qkv_width] = contract(input_ref[:, here], lin_ref[...], 0, 0).astype(bf16)
            out_ref[rows, qkv_width:] = contract(grad_ref[:, here], rows_ref[...], 0, 0).astype(bf16)

    def attn_products(inputs, lin, grads, rows):
        if shard % 16:
            return jnp.concatenate(
                [
                    contract(columns_out(inputs), lin, 0, 0),
                    contract(columns_out(grads), rows, 0, 0),
                ],
                axis=1,
            ).astype(bf16)
        return pl.pallas_call(
            products_kernel,
            in_specs=[SCALARS] + [WHOLE] * 4,
            out_specs=WHOLE,
            out_shape=shape_of((width, qkv_width + query_width), bf16),
            compiler_params=pltpu.CompilerParams(vmem_limit_bytes=VMEM_BYTES),
            name="attn_products",
        )(me[None], inputs, lin, grads, rows)

    gate_up = rows_of_all(jnp.concatenate([w_gate, w_up], axis=1))
    down_w = rows_of_all(w_down)
    attn_own = jnp.concatenate([w_query, w_key, w_value, w_out], axis=1)
    own_gains = jnp.stack([norm_attn_out, norm_ffn_in, norm_ffn_out, norm_attn_in])
    gain_rows = jnp.zeros((16, attn_own.shape[1]), bf16).at[:4, :shard].set(own_gains)
    from_a, from_b, top, bottom = spread_far(jnp.concatenate([attn_own, gain_rows], axis=0))
    attn_w = spread_near(
        jnp.concatenate([attn_own, from_a[:shard], from_b[:shard], top, bottom], axis=0)
    )
    qkv_w = [block[:, :qkv_width] for block in attn_w]
    out_w = [block[:, qkv_width:] for block in attn_w]
    gain_a, gain_b = (held[shard : shard + 4, :shard] for held in (from_a, from_b))
    gains = jnp.concatenate(
        spread_near(
            jnp.concatenate([own_gains, gain_a, gain_b, swap(gain_b, far_a)], axis=1)
        ),
        axis=1,
    )
    all_gains = columns_out(gains).astype(f32)
    gain_two, gain_three, gain_four, gain_one = jnp.split(all_gains, 4)

    tok_float = rows_in(tokens).astype(f32)
    own_cot = lax.dynamic_slice_in_dim(cotangent, my_layer * own_rows, own_rows, 0).astype(f32)
    own_tok = tok_float[:own_rows]
    attn_input = lax.optimization_barrier(
        (
            columns_in(rows_in(tokens)).astype(f32) * rms_scale(tok_float) * gains[3:].astype(f32)
        ).astype(bf16)
    )
    lin = times_rows(attn_input, qkv_w)
    row_place = jnp.concatenate(
        [
            (my_layer ^ step) * own_rows + jnp.arange(own_rows, dtype=jnp.int32)
            for step in range(layers)
        ]
    )
    query_pos = me * tok_rows + row_place
    half_width = HD // 2
    frequency = jnp.exp(jnp.arange(half_width, dtype=f32) * (-2.0 * math.log(10000.0) / HD))
    angles = query_pos.astype(f32)[:, None] * frequency[None, :]
    cos_table, sine_table = jnp.cos(angles)[:, None, :], jnp.sin(angles)[:, None, :]
    queries = (
        rotate(lin[:, :query_width].reshape(tok_rows, heads_local, HD), cos_table, sine_table)
        * HD ** (-0.5)
    ).astype(bf16)
    assert key_heads == 1
    query_rows = queries.reshape(tok_rows, heads_local, HD).transpose(1, 0, 2).reshape(-1, HD)
    keys_rot = (
        rotate(
            lin[:, query_width : query_width + key_width].reshape(tok_rows, key_heads, HD),
            cos_table,
            sine_table,
        )
        .astype(bf16)
        .reshape(tok_rows, key_width)
    )
    values_b = lin[:, query_width + key_width :].astype(bf16)
    pair = jnp.concatenate([keys_rot, values_b], axis=1)
    pair_far = jnp.concatenate(
        [pair] + [swap(pair, step) for step in (far_a, far_b, far_a | far_b)], axis=0
    )
    pairs = jnp.concatenate(spread_near(pair_far), axis=0)
    key_count = pairs.shape[0]
    key_places = jnp.concatenate([(me ^ block) * tok_rows + row_place for block in order])[None, :]
    places = jnp.tile(query_pos, heads_local)[:, None]
    attn_float, attn_rows, attn_log = attend(query_rows, pairs, places, key_places, heads_local)
    parts, _, _ = layer_scatter(times_rows_t(attn_rows, out_w).astype(bf16))
    if in_kernels:
        attn_total, hidden_res, own_input = on_own_rows(
            residual_body,
            *parts,
            (own_tok, all_gains),
            [(own_rows, f32), (own_rows, f32), (own_rows, bf16)],
            "residual",
        )
    else:
        attn_total = columns_out(sum_of(parts))
        hidden_res = own_tok + attn_total * rms_scale(attn_total) * gain_two
        own_input = (hidden_res * rms_scale(hidden_res) * gain_three).astype(bf16)
    pieces, _, _ = layer_gather(own_input)
    ffn_input = jnp.concatenate(pieces, axis=0)

    both_lin = product(ffn_input, gate_up)
    gate_lin, up_lin = both_lin[:, :ffn_width], both_lin[:, ffn_width:]
    activated, gelu_pull = jax.vjp(gelu_tanh, gate_lin)
    hidden_b = (activated * up_lin).astype(bf16)
    if gather_factors:
        all_hidden = rows_of_all(hidden_b)
    parts, _, _ = layer_scatter(contract(hidden_b, down_w, 1, 1).astype(bf16))
    if in_kernels:
        own_output, own_grad_ffn, grad_gain_four = on_own_rows(
            output_body,
            *parts,
            (hidden_res, own_cot, all_gains),
            [(own_rows, bf16), (own_rows, bf16), (1, f32)],
            "output",
            scratch=0,
        )
    else:
        ffn_total = sum_of(parts)
        inv_four = rms_scale(ffn_total)
        normed_four = ffn_total * inv_four
        own_output = (hidden_res + normed_four * gain_four).astype(bf16)
        grad_gain_four = jnp.sum(own_cot * normed_four, axis=0, keepdims=True)
        own_grad_ffn = norm_back(inv_four, normed_four, own_cot * gain_four).astype(bf16)

    pieces, _, _ = layer_gather(own_grad_ffn)
    grad_ffn = jnp.concatenate(pieces, axis=0)
    if gather_factors:
        own_columns = lax.all_to_all(
            columns_by_owner(own_input, own_grad_ffn),
            "ctx",
            split_axis=0,
            concat_axis=0,
            tiled=True,
        )
    sent_output = after(own_output, grad_ffn)
    if layers == 4:
        output_pieces = [own_output, swap(sent_output, 1, "tp"), swap(sent_output, 2, "tp")]
    else:
        output_pieces, _, _ = layer_gather(sent_output)
    grad_hidden = product(grad_ffn, down_w)
    grad_gate = gelu_pull(grad_hidden * up_lin)[0].astype(bf16)
    grad_up = (grad_hidden * activated).astype(bf16)
    grad_both = jnp.concatenate([grad_gate, grad_up], axis=1)
    if gather_factors:
        all_both = rows_of_all(after(grad_both, all_hidden))
    else:
        grad_w_down = sum_scatter(contract(grad_ffn, hidden_b, 0, 0))
        grad_w_both = sum_scatter(contract(ffn_input, grad_both, 0, 0))
        grad_w_gate, grad_w_up = grad_w_both[:, :ffn_width], grad_w_both[:, ffn_width:]
    grad_in_part = contract(grad_both, gate_up, 1, 1).astype(bf16)
    grad_in_part = after(grad_in_part, *output_pieces[1:])
    parts, _, _ = layer_scatter(grad_in_part)
    if in_kernels:
        grad_res, own_grad_attn, grad_gain_two = on_own_rows(
            residual_back_body,
            *parts,
            (hidden_res, attn_total, own_cot, all_gains),
            [(own_rows, f32), (own_rows, bf16), (1, f32)],
            "residual_back",
            scratch=2,
        )
    else:
        inv_three = rms_scale(hidden_res)
        grad_res = own_cot + norm_back(
            inv_three, hidden_res * inv_three, sum_of(parts) * gain_three
        )
        inv_two = rms_scale(attn_total)
        normed_two = attn_total * inv_two
        grad_gain_two = jnp.sum(grad_res * normed_two, axis=0, keepdims=True)
        own_grad_attn = norm_back(inv_two, normed_two, grad_res * gain_two)
        own_grad_attn = columns_in(own_grad_attn.astype(bf16))

    pieces, _, _ = layer_gather(own_grad_attn)
    grad_attn = jnp.concatenate(pieces, axis=0)
    grad_rows = times_rows(grad_attn, out_w).astype(bf16)
    grad_heads = grad_rows.reshape(tok_rows, heads_local, HD).transpose(1, 0, 2).reshape(-1, HD)
    grad_q, pair_grad = attend_back(
        query_rows, grad_heads, attn_float, attn_log, pairs, places, key_places
    )
    if gather_factors:
        pair_grad = after(pair_grad, own_columns)
        columns_then = after(own_columns, grad_attn)
        if layers == 4:
            column_pieces = [columns_then] + [swap(columns_then, bit, "tp") for bit in (1, 2)]
        else:
            column_pieces, _, _ = layer_gather(columns_then)
    near_rows = 4 * tok_rows
    pair_part = [
        pair_grad[start : start + near_rows] for start in range(0, key_count, near_rows)
    ]
    for bit in reversed(near):
        half = len(pair_part) // 2
        pair_part = [
            (kept.astype(f32) + swap(sent, bit).astype(f32)).astype(bf16)
            for kept, sent in zip(pair_part[:half], pair_part[half:])
        ]
    pair_part = pair_part[0]
    if layers == 4:
        output_pieces.append(swap(after(output_pieces[2], grad_rows), 1, "tp"))
    arrived = [
        swap(pair_part[index * tok_rows : (index + 1) * tok_rows], step)
        for index, step in ((1, far_a), (2, far_b), (3, far_a | far_b))
    ]
    pair_own = after(pair_part[:tok_rows], output_pieces[3]).astype(f32)
    for piece in arrived:
        pair_own = pair_own + piece.astype(f32)
    if gather_factors:
        if layers == 4:
            column_pieces.append(swap(after(column_pieces[2], arrived[0]), 1, "tp"))
    grad_query_lin = (
        rotate(
            grad_q.reshape(heads_local, tok_rows, HD).transpose(1, 0, 2), cos_table, -sine_table
        )
        * HD ** (-0.5)
    ).reshape(tok_rows, query_width)
    grad_key_lin = rotate(
        pair_own[:, :key_width].reshape(tok_rows, key_heads, HD), cos_table, -sine_table
    ).reshape(tok_rows, key_width)
    grad_lin = jnp.concatenate(
        [grad_query_lin, grad_key_lin, pair_own[:, key_width:]], axis=1
    ).astype(bf16)
    partial = attn_products(
        attn_input,
        after(grad_lin, all_both) if gather_factors else grad_lin,
        grad_attn,
        attn_rows,
    )
    attn_sums = sum_scatter(partial)
    grad_w_lin, grad_w_out = attn_sums[:, :qkv_width], attn_sums[:, qkv_width:]
    grad_in_part = times_rows_t(after(grad_lin, partial), qkv_w).astype(bf16)

    if gather_factors:
        columns = jnp.stack([after(piece, grad_in_part) for piece in column_pieces], axis=1)
        columns = columns.reshape(tok_rows * ring, 2 * shard)
        ffn_cols, down_cols = columns[:, :shard], columns[:, shard:]

    def gate_gradient(then):
        return (contract(after(ffn_cols, then), all_both[:, :ffn_width], 0, 0),)

    if gather_factors:
        parts, _, (grad_w_gate,) = layer_scatter(grad_in_part, None, gate_gradient)
    else:
        parts, _, _ = layer_scatter(grad_in_part)
    if in_kernels:
        own_grad, grad_gain_one = on_own_rows(
            token_back_body,
            *parts,
            (own_tok, grad_res, all_gains),
            [(own_rows, bf16), (1, f32)],
            "token_back",
            scratch=2,
        )
    else:
        grad_attn_in = columns_out(sum_of(parts))
        own_inv = rms_scale(own_tok)
        own_normed = own_tok * own_inv
        own_grad = grad_res + norm_back(own_inv, own_normed, grad_attn_in * gain_one)
        own_grad = own_grad.astype(bf16)
        grad_gain_one = jnp.sum(grad_attn_in * own_normed, axis=0, keepdims=True)
    token_pieces, _, _ = layer_gather(own_grad)
    if gather_factors:
        grad_w_up = contract(after(ffn_cols, own_grad), all_both[:, ffn_width:], 0, 0)
        grad_w_down = contract(after(down_cols, token_pieces[2], grad_w_up), all_hidden, 0, 0)
    grad_tokens = rows_out(token_pieces).astype(f32)
    output = rows_out([after(output_pieces[0], token_pieces[3])] + output_pieces[1:])

    third_gain = norm_ffn_in.astype(f32)
    gain_third = (
        jnp.sum(w_gate.astype(f32) * grad_w_gate + w_up.astype(f32) * grad_w_up, axis=1)
        / third_gain
    )[None, :]
    gain_sum = columns_in(
        jnp.concatenate([grad_gain_one, grad_gain_two, grad_gain_four], axis=0)
    )
    gain_sum = after(gain_sum, token_pieces[1])
    for bit in reversed(near):
        half = gain_sum.shape[1] // 2
        gain_sum = gain_sum[:, :half] + swap(gain_sum[:, half:], bit)
    own_gain = gain_sum[:, :shard]
    for index, step in ((1, far_a), (2, far_b), (3, far_a | far_b)):
        own_gain = own_gain + swap(gain_sum[:, index * shard : (index + 1) * shard], step)
    own_gain = jnp.concatenate([own_gain, gain_third], axis=0)
    for bit in [1 << index for index in range(layers.bit_length() - 1)]:
        own_gain = own_gain + swap(own_gain, bit, "tp")
    return (
        output,
        grad_tokens,
        grad_w_lin[:, :query_width],
        grad_w_lin[:, query_width : query_width + key_width],
        grad_w_lin[:, query_width + key_width :],
        grad_w_out,
        grad_w_gate,
        grad_w_up,
        grad_w_down,
        own_gain[0],
        own_gain[1],
        own_gain[3],
        own_gain[2],
    )


def solution(mesh):
    rows, block = P("ctx", None), P("ctx", "tp")
    gain = P("ctx")
    return jax.shard_map(
        local,
        mesh=mesh,
        in_specs=(rows,) + (block,) * 7 + (gain,) * 4 + (rows,),
        out_specs=(rows, rows) + (block,) * 7 + (gain,) * 4,
        check_vma=False,
    )
```

```python
import functools
import math

import jax
import jax.numpy as jnp
from jax import lax
from jax.experimental import pallas as pl
from jax.experimental.pallas import tpu as pltpu
from jax.sharding import PartitionSpec as P

HD = 256


EPSILON = 1e-06
SOFT_CAP = 50.0
MASKED = -1e30

bf16, f32 = jnp.bfloat16, jnp.float32


def rms_scale(values):
    return lax.rsqrt(jnp.mean(values * values, axis=-1, keepdims=True) + EPSILON)


def norm_back(inv_rms, normed, gradient):
    return inv_rms * (gradient - normed * jnp.mean(gradient * normed, axis=-1, keepdims=True))


def rotate(values, cos_table, sine_table):
    half_width = values.shape[-1] // 2
    leading = values[..., :half_width]
    trailing = values[..., half_width:]
    return jnp.concatenate(
        [leading * cos_table - trailing * sine_table, trailing * cos_table + leading * sine_table],
        axis=-1,
    )


def gelu_tanh(values):
    return jax.nn.gelu(values, approximate=True)


def product(first_operand, second_operand):
    return jnp.dot(first_operand, second_operand, preferred_element_type=f32)


def contract(first_operand, second_operand, first_dim, second_dim):
    return lax.dot_general(
        first_operand,
        second_operand,
        (((first_dim,), (second_dim,)), ((), ())),
        preferred_element_type=f32,
    )


def after(value, *earlier):
    return lax.optimization_barrier((value,) + earlier)[0]


def swap(value, bit, axis="ctx"):
    count = lax.axis_size(axis)
    return lax.ppermute(value, axis, [(index, index ^ bit) for index in range(count)])


WHOLE = pl.BlockSpec(memory_space=pltpu.VMEM)
SCALARS = pl.BlockSpec(memory_space=pltpu.SMEM)
VMEM_BYTES = 24 * 2**20


def shape_of(dims, kind):
    return jax.ShapeDtypeStruct(dims, kind)


def key_block(key_count):
    return math.gcd(key_count, 512)


def attend_kernel(steps, group, query_ref, pair_ref, place_ref, key_place_ref, out_ref, rows_ref, log_ref):
    step = pl.program_id(0)
    rows = place_ref.shape[0]

    @pl.when(step == 0)
    def _():
        out_ref[...] = jnp.zeros_like(out_ref)
        log_ref[...] = jnp.zeros_like(log_ref)

    keys, values = pair_ref[:, :HD], pair_ref[:, HD:]
    scores = contract(query_ref[...], keys, 1, 1)
    capped = SOFT_CAP * jnp.tanh(scores * (1.0 / SOFT_CAP))
    visible = key_place_ref[...] <= place_ref[...]
    weights = jnp.where(visible, jnp.exp(capped), 0.0)
    log_ref[...] += jnp.sum(weights, axis=-1, keepdims=True)
    out_ref[...] += product(weights.astype(bf16), values)

    @pl.when(step == steps - 1)
    def _():
        total = log_ref[...]
        result = out_ref[...] / total
        out_ref[...] = result
        log_ref[...] = jnp.log(total)
        each = rows // group
        for head in range(group):
            rows_ref[:, head * HD : (head + 1) * HD] = result[head * each : (head + 1) * each].astype(bf16)


def attend(queries, pairs, places, key_places, group):
    rows, key_count = queries.shape[0], pairs.shape[0]
    block = key_block(key_count)
    steps = key_count // block
    fixed = lambda step: (0, 0)
    return pl.pallas_call(
        functools.partial(attend_kernel, steps, group),
        grid=(steps,),
        in_specs=[
            pl.BlockSpec((rows, HD), fixed),
            pl.BlockSpec((block, 2 * HD), lambda step: (step, 0)),
            pl.BlockSpec((rows, 1), fixed),
            pl.BlockSpec((1, block), lambda step: (0, step)),
        ],
        out_specs=[
            pl.BlockSpec((rows, HD), fixed),
            pl.BlockSpec((rows // group, group * HD), fixed),
            pl.BlockSpec((rows, 1), fixed),
        ],
        out_shape=[
            shape_of((rows, HD), f32),
            shape_of((rows // group, group * HD), bf16),
            shape_of((rows, 1), f32),
        ],
        compiler_params=pltpu.CompilerParams(vmem_limit_bytes=VMEM_BYTES),
        name="attend",
    )(queries, pairs, places, key_places)


def attend_back_kernel(
    query_ref, grad_ref, out_ref, log_ref, pair_ref, place_ref, key_place_ref, query_grad_ref, pair_grad_ref, delta_ref
):
    @pl.when(pl.program_id(0) == 0)
    def _():
        query_grad_ref[...] = jnp.zeros_like(query_grad_ref)
        delta_ref[...] = jnp.sum(grad_ref[...].astype(f32) * out_ref[...], axis=-1, keepdims=True)

    queries, grads = query_ref[...], grad_ref[...]
    keys, values = pair_ref[:, :HD], pair_ref[:, HD:]
    part = jnp.tanh(contract(queries, keys, 1, 1) * (1.0 / SOFT_CAP))
    visible = key_place_ref[...] <= place_ref[...]
    probs = jnp.where(visible, jnp.exp(SOFT_CAP * part - log_ref[...]), 0.0)
    pair_grad_ref[:, HD:] = contract(probs.astype(bf16), grads, 0, 0).astype(bf16)
    slope = contract(grads, values, 1, 1) - delta_ref[...]
    score_grad = (probs * slope * (1.0 - part * part)).astype(bf16)
    query_grad_ref[...] += product(score_grad, keys)
    pair_grad_ref[:, :HD] = contract(score_grad, queries, 0, 0).astype(bf16)


def attend_back(queries, grads, outs, logs, pairs, places, key_places):
    rows, key_count = queries.shape[0], pairs.shape[0]
    block = key_block(key_count)
    fixed = lambda step: (0, 0)
    tall = pl.BlockSpec((rows, HD), fixed)
    column = pl.BlockSpec((rows, 1), fixed)
    moving = pl.BlockSpec((block, 2 * HD), lambda step: (step, 0))
    return pl.pallas_call(
        attend_back_kernel,
        grid=(key_count // block,),
        in_specs=[tall, tall, tall, column, moving, column, pl.BlockSpec((1, block), lambda step: (0, step))],
        out_specs=[tall, moving],
        out_shape=[shape_of((rows, HD), f32), shape_of((key_count, 2 * HD), bf16)],
        scratch_shapes=[pltpu.VMEM((rows, 1), f32)],
        compiler_params=pltpu.CompilerParams(vmem_limit_bytes=VMEM_BYTES),
        name="attend_back",
    )(queries, grads, outs, logs, pairs, places, key_places)


def local(
    tokens,
    w_query,
    w_key,
    w_value,
    w_out,
    w_gate,
    w_up,
    w_down,
    norm_attn_in,
    norm_attn_out,
    norm_ffn_in,
    norm_ffn_out,
    cotangent,
):
    tok_rows, width = tokens.shape
    heads_local = w_query.shape[1] // HD
    key_heads = w_key.shape[1] // HD
    query_width = heads_local * HD
    key_width = key_heads * HD
    qkv_width = query_width + 2 * key_width
    ffn_width = w_gate.shape[1]
    ring = lax.axis_size("ctx")
    layers = lax.axis_size("tp")
    me = lax.axis_index("ctx")
    my_layer = lax.axis_index("tp")
    shard = width // ring
    own_rows = tok_rows // layers
    upper = shard // 32 * 16
    far_a, far_b = ring // 4, ring // 2
    near = [1 << bit for bit in range(far_a.bit_length() - 1)]
    order = [0, far_a, far_b, far_a | far_b]
    for bit in near:
        order = order + [block | bit for block in order]
    near_width = 4 * shard
    gather_factors = tok_rows * ring <= width

    def spread_far(piece):
        from_a, from_b = swap(piece, far_a), swap(piece, far_b)
        return from_a, from_b, swap(from_b[:upper], far_a), swap(from_a[upper:shard], far_b)

    def spread_near(block):
        blocks = [block]
        for bit in near:
            blocks = blocks + [swap(held, bit) for held in blocks]
        return blocks

    def by_near(array):
        return [array[:, start : start + near_width] for start in range(0, width, near_width)]

    def times_rows(activation, blocks):
        total = None
        for part, block in zip(by_near(activation), blocks):
            term = product(part, block)
            total = term if total is None else total + term
        return total

    def times_rows_t(activation, blocks):
        return jnp.concatenate([contract(activation, block, 1, 1) for block in blocks], axis=1)

    def layer_scatter(partial, first=None, second=None):
        pieces = [partial[step * own_rows : (step + 1) * own_rows] for step in range(layers)]
        done_first = first(partial) if first else ()
        if layers == 4:
            passed_on = swap(pieces[3], 1, "tp")
            arrived = [swap(pieces[1], 1, "tp")]
            held = after(pieces[2], *done_first) if first else pieces[2]
            pair_sum = (held.astype(f32) + passed_on.astype(f32)).astype(bf16)
            arrived.append(swap(pair_sum, 2, "tp"))
        else:
            pair_sum = partial
            arrived = [swap(pieces[step], step, "tp") for step in range(1, layers)]
        done_second = second(pair_sum) if second else ()
        if done_first or done_second:
            arrived[0] = after(arrived[0], *done_first, *done_second)
        return (partial, arrived), done_first, done_second

    def sum_of(parts):
        partial, arrived = parts
        total = partial[:own_rows].astype(f32)
        for piece in arrived:
            total = total + piece.astype(f32)
        return total

    def layer_gather(rows, first=None, second=None):
        done_first = first(rows) if first else ()
        if layers == 4:
            across = swap(rows, 2, "tp")
            beside = swap(rows, 1, "tp")
            across_then = after(across, *done_first) if first else across
            pieces = [rows, beside, across, swap(across_then, 1, "tp")]
        else:
            across_then = rows
            pieces = [rows] + [swap(rows, step, "tp") for step in range(1, layers)]
        done_second = second(across_then) if second else ()
        if first or second:
            pieces[0] = after(pieces[0], *done_first, *done_second)
        return pieces, done_first, done_second

    def rows_in(array):
        return jnp.concatenate(
            [
                lax.dynamic_slice_in_dim(array, (my_layer ^ step) * own_rows, own_rows, 0)
                for step in range(layers)
            ],
            axis=0,
        )

    def rows_out(pieces):
        result = jnp.zeros((tok_rows,) + pieces[0].shape[1:], pieces[0].dtype)
        for step, piece in enumerate(pieces):
            result = lax.dynamic_update_slice_in_dim(
                result, piece, (my_layer ^ step) * own_rows, 0
            )
        return result

    def columns_in(array):
        return jnp.concatenate(
            [lax.dynamic_slice_in_dim(array, (me ^ block) * shard, shard, 1) for block in order],
            axis=1,
        )

    def columns_out(array):
        def place(block):
            found = (block & far_a) // far_a + 2 * ((block & far_b) // far_b)
            for index, bit in enumerate(near):
                found = found + (4 << index) * ((block & bit) // bit)
            return found

        return jnp.concatenate(
            [
                lax.dynamic_slice_in_dim(array, place(me ^ block) * shard, shard, 1)
                for block in range(ring)
            ],
            axis=1,
        )

    def rows_of_all(array):
        return lax.all_gather(array, "ctx", axis=0, tiled=True)

    def in_order(me_ref, source_ref, target_ref, inverse):
        for index in range(ring):

            @pl.when(me_ref[0] == index)
            def _():
                for place, block in enumerate(order):
                    here = slice(place * shard, (place + 1) * shard)
                    there = slice((index ^ block) * shard, ((index ^ block) + 1) * shard)
                    if inverse:
                        target_ref[:, there] = source_ref[:, here]
                    else:
                        target_ref[:, here] = source_ref[:, there]

    in_kernels = ring <= 8 and own_rows % 16 == 0 and layers == 4

    def on_own_rows(body, partial, arrived, others, outs, name, scratch=1):
        def kernel(me_ref, part_ref, one_ref, two_ref, *refs):
            total = part_ref[...].astype(f32) + one_ref[...].astype(f32) + two_ref[...].astype(f32)
            body(me_ref, total, *refs)

        wide = pl.BlockSpec((own_rows, width), lambda step: (0, 0))
        return pl.pallas_call(
            kernel,
            grid=(1,),
            in_specs=[SCALARS, wide] + [WHOLE] * (2 + len(others)),
            out_specs=[WHOLE] * len(outs),
            out_shape=[shape_of((rows, width), kind) for rows, kind in outs],
            scratch_shapes=[pltpu.VMEM((own_rows, width), f32)] * scratch,
            compiler_params=pltpu.CompilerParams(vmem_limit_bytes=VMEM_BYTES),
            name=name,
        )(me[None], partial, *arrived, *others)

    def residual_body(me_ref, total, tok_ref, gain_ref, attn_ref, hidden_ref, input_ref, held_ref):
        held_ref[...] = total
        in_order(me_ref, held_ref, attn_ref, True)
        attn = attn_ref[...]
        hidden = tok_ref[...] + attn * rms_scale(attn) * gain_ref[0:1, :]
        hidden_ref[...] = hidden
        input_ref[...] = (hidden * rms_scale(hidden) * gain_ref[1:2, :]).astype(bf16)

    def output_body(me_ref, total, hidden_ref, cot_ref, gain_ref, out_ref, grad_ref, gain_grad_ref):
        inverse = rms_scale(total)
        normed = total * inverse
        gain, cot = gain_ref[2:3, :], cot_ref[...]
        out_ref[...] = (hidden_ref[...] + normed * gain).astype(bf16)
        gain_grad_ref[...] = jnp.sum(cot * normed, axis=0, keepdims=True)
        grad_ref[...] = norm_back(inverse, normed, cot * gain).astype(bf16)

    def residual_back_body(
        me_ref, total, hidden_ref, attn_ref, cot_ref, gain_ref, res_ref, grad_ref, gain_grad_ref, held_ref, moved_ref
    ):
        hidden, attn = hidden_ref[...], attn_ref[...]
        inverse = rms_scale(hidden)
        res = cot_ref[...] + norm_back(inverse, hidden * inverse, total * gain_ref[1:2, :])
        res_ref[...] = res
        inverse = rms_scale(attn)
        normed = attn * inverse
        gain_grad_ref[...] = jnp.sum(res * normed, axis=0, keepdims=True)
        held_ref[...] = norm_back(inverse, normed, res * gain_ref[0:1, :])
        in_order(me_ref, held_ref, moved_ref, False)
        grad_ref[...] = moved_ref[...].astype(bf16)

    def token_back_body(me_ref, total, tok_ref, res_ref, gain_ref, grad_ref, gain_grad_ref, held_ref, moved_ref):
        held_ref[...] = total
        in_order(me_ref, held_ref, moved_ref, True)
        tok, grad = tok_ref[...], moved_ref[...]
        inverse = rms_scale(tok)
        normed = tok * inverse
        gain_grad_ref[...] = jnp.sum(grad * normed, axis=0, keepdims=True)
        grad_ref[...] = (
            res_ref[...] + norm_back(inverse, normed, grad * gain_ref[3:4, :])
        ).astype(bf16)

    def by_owner_kernel(first_ref, second_ref, out_ref):
        for block in range(ring):
            here = slice(block * shard, (block + 1) * shard)
            out_ref[block, :, :shard] = first_ref[:, here]
            out_ref[block, :, shard:] = second_ref[:, here]

    def columns_by_owner(first, second):
        rows = first.shape[0]
        if not in_kernels:
            stacked = jnp.stack([array.reshape(rows, ring, shard) for array in (first, second)])
            return stacked.transpose(2, 1, 0, 3).reshape(ring, rows, 2 * shard)
        return pl.pallas_call(
            by_owner_kernel,
            in_specs=[WHOLE] * 2,
            out_specs=WHOLE,
            out_shape=shape_of((ring, rows, 2 * shard), bf16),
            compiler_params=pltpu.CompilerParams(vmem_limit_bytes=VMEM_BYTES),
            name="by_owner",
        )(first, second)

    def sum_scatter(partial):
        return lax.psum_scatter(
            partial.astype(bf16), "ctx", scatter_dimension=0, tiled=True
        ).astype(f32)

    def products_kernel(me_ref, input_ref, lin_ref, grad_ref, rows_ref, out_ref):
        for place, block in enumerate(order):
            rows = pl.ds(pl.multiple_of((me_ref[0] ^ block) * shard, 16), shard)
            here = slice(place * shard, (place + 1) * shard)
            out_ref[rows, :qkv_width] = contract(input_ref[:, here], lin_ref[...], 0, 0).astype(bf16)
            out_ref[rows, qkv_width:] = contract(grad_ref[:, here], rows_ref[...], 0, 0).astype(bf16)

    def attn_products(inputs, lin, grads, rows):
        if shard % 16:
            return jnp.concatenate(
                [
                    contract(columns_out(inputs), lin, 0, 0),
                    contract(columns_out(grads), rows, 0, 0),
                ],
                axis=1,
            ).astype(bf16)
        return pl.pallas_call(
            products_kernel,
            in_specs=[SCALARS] + [WHOLE] * 4,
            out_specs=WHOLE,
            out_shape=shape_of((width, qkv_width + query_width), bf16),
            compiler_params=pltpu.CompilerParams(vmem_limit_bytes=VMEM_BYTES),
            name="attn_products",
        )(me[None], inputs, lin, grads, rows)

    gate_up = rows_of_all(jnp.concatenate([w_gate, w_up], axis=1))
    down_w = rows_of_all(w_down)
    attn_own = jnp.concatenate([w_query, w_key, w_value, w_out], axis=1)
    own_gains = jnp.stack([norm_attn_out, norm_ffn_in, norm_ffn_out, norm_attn_in])
    gain_rows = jnp.zeros((16, attn_own.shape[1]), bf16).at[:4, :shard].set(own_gains)
    from_a, from_b, top, bottom = spread_far(jnp.concatenate([attn_own, gain_rows], axis=0))
    attn_w = spread_near(
        jnp.concatenate([attn_own, from_a[:shard], from_b[:shard], top, bottom], axis=0)
    )
    qkv_w = [block[:, :qkv_width] for block in attn_w]
    out_w = [block[:, qkv_width:] for block in attn_w]
    gain_a, gain_b = (held[shard : shard + 4, :shard] for held in (from_a, from_b))
    gains = jnp.concatenate(
        spread_near(
            jnp.concatenate([own_gains, gain_a, gain_b, swap(gain_b, far_a)], axis=1)
        ),
        axis=1,
    )
    all_gains = columns_out(gains).astype(f32)
    gain_two, gain_three, gain_four, gain_one = jnp.split(all_gains, 4)

    tok_float = rows_in(tokens).astype(f32)
    own_cot = lax.dynamic_slice_in_dim(cotangent, my_layer * own_rows, own_rows, 0).astype(f32)
    own_tok = tok_float[:own_rows]
    attn_input = lax.optimization_barrier(
        (
            columns_in(rows_in(tokens)).astype(f32) * rms_scale(tok_float) * gains[3:].astype(f32)
        ).astype(bf16)
    )
    lin = times_rows(attn_input, qkv_w)
    row_place = jnp.concatenate(
        [
            (my_layer ^ step) * own_rows + jnp.arange(own_rows, dtype=jnp.int32)
            for step in range(layers)
        ]
    )
    query_pos = me * tok_rows + row_place
    half_width = HD // 2
    frequency = jnp.exp(jnp.arange(half_width, dtype=f32) * (-2.0 * math.log(10000.0) / HD))
    angles = query_pos.astype(f32)[:, None] * frequency[None, :]
    cos_table, sine_table = jnp.cos(angles)[:, None, :], jnp.sin(angles)[:, None, :]
    queries = (
        rotate(lin[:, :query_width].reshape(tok_rows, heads_local, HD), cos_table, sine_table)
        * HD ** (-0.5)
    ).astype(bf16)
    assert key_heads == 1
    query_rows = queries.reshape(tok_rows, heads_local, HD).transpose(1, 0, 2).reshape(-1, HD)
    keys_rot = (
        rotate(
            lin[:, query_width : query_width + key_width].reshape(tok_rows, key_heads, HD),
            cos_table,
            sine_table,
        )
        .astype(bf16)
        .reshape(tok_rows, key_width)
    )
    values_b = lin[:, query_width + key_width :].astype(bf16)
    pair = jnp.concatenate([keys_rot, values_b], axis=1)
    pair_far = jnp.concatenate(
        [pair] + [swap(pair, step) for step in (far_a, far_b, far_a | far_b)], axis=0
    )
    pairs = jnp.concatenate(spread_near(pair_far), axis=0)
    key_count = pairs.shape[0]
    key_places = jnp.concatenate([(me ^ block) * tok_rows + row_place for block in order])[None, :]
    places = jnp.tile(query_pos, heads_local)[:, None]
    attn_float, attn_rows, attn_log = attend(query_rows, pairs, places, key_places, heads_local)
    parts, _, _ = layer_scatter(times_rows_t(attn_rows, out_w).astype(bf16))
    if in_kernels:
        attn_total, hidden_res, own_input = on_own_rows(
            residual_body,
            *parts,
            (own_tok, all_gains),
            [(own_rows, f32), (own_rows, f32), (own_rows, bf16)],
            "residual",
        )
    else:
        attn_total = columns_out(sum_of(parts))
        hidden_res = own_tok + attn_total * rms_scale(attn_total) * gain_two
        own_input = (hidden_res * rms_scale(hidden_res) * gain_three).astype(bf16)
    pieces, _, _ = layer_gather(own_input)
    ffn_input = jnp.concatenate(pieces, axis=0)

    both_lin = product(ffn_input, gate_up)
    gate_lin, up_lin = both_lin[:, :ffn_width], both_lin[:, ffn_width:]
    activated, gelu_pull = jax.vjp(gelu_tanh, gate_lin)
    hidden_b = (activated * up_lin).astype(bf16)
    if gather_factors:
        all_hidden = rows_of_all(hidden_b)
    parts, _, _ = layer_scatter(contract(hidden_b, down_w, 1, 1).astype(bf16))
    if in_kernels:
        own_output, own_grad_ffn, grad_gain_four = on_own_rows(
            output_body,
            *parts,
            (hidden_res, own_cot, all_gains),
            [(own_rows, bf16), (own_rows, bf16), (1, f32)],
            "output",
            scratch=0,
        )
    else:
        ffn_total = sum_of(parts)
        inv_four = rms_scale(ffn_total)
        normed_four = ffn_total * inv_four
        own_output = (hidden_res + normed_four * gain_four).astype(bf16)
        grad_gain_four = jnp.sum(own_cot * normed_four, axis=0, keepdims=True)
        own_grad_ffn = norm_back(inv_four, normed_four, own_cot * gain_four).astype(bf16)

    pieces, _, _ = layer_gather(own_grad_ffn)
    grad_ffn = jnp.concatenate(pieces, axis=0)
    if gather_factors:
        own_columns = lax.all_to_all(
            columns_by_owner(own_input, own_grad_ffn),
            "ctx",
            split_axis=0,
            concat_axis=0,
            tiled=True,
        )
    sent_output = after(own_output, grad_ffn)
    if layers == 4:
        output_pieces = [own_output, swap(sent_output, 1, "tp"), swap(sent_output, 2, "tp")]
    else:
        output_pieces, _, _ = layer_gather(sent_output)
    grad_hidden = product(grad_ffn, down_w)
    grad_gate = gelu_pull(grad_hidden * up_lin)[0].astype(bf16)
    grad_up = (grad_hidden * activated).astype(bf16)
    grad_both = jnp.concatenate([grad_gate, grad_up], axis=1)
    if gather_factors:
        all_both = rows_of_all(after(grad_both, all_hidden))
    else:
        grad_w_down = sum_scatter(contract(grad_ffn, hidden_b, 0, 0))
        grad_w_both = sum_scatter(contract(ffn_input, grad_both, 0, 0))
        grad_w_gate, grad_w_up = grad_w_both[:, :ffn_width], grad_w_both[:, ffn_width:]
    grad_in_part = contract(grad_both, gate_up, 1, 1).astype(bf16)
    grad_in_part = after(grad_in_part, *output_pieces[1:])
    parts, _, _ = layer_scatter(grad_in_part)
    if in_kernels:
        grad_res, own_grad_attn, grad_gain_two = on_own_rows(
            residual_back_body,
            *parts,
            (hidden_res, attn_total, own_cot, all_gains),
            [(own_rows, f32), (own_rows, bf16), (1, f32)],
            "residual_back",
            scratch=2,
        )
    else:
        inv_three = rms_scale(hidden_res)
        grad_res = own_cot + norm_back(
            inv_three, hidden_res * inv_three, sum_of(parts) * gain_three
        )
        inv_two = rms_scale(attn_total)
        normed_two = attn_total * inv_two
        grad_gain_two = jnp.sum(grad_res * normed_two, axis=0, keepdims=True)
        own_grad_attn = norm_back(inv_two, normed_two, grad_res * gain_two)
        own_grad_attn = columns_in(own_grad_attn.astype(bf16))

    pieces, _, _ = layer_gather(own_grad_attn)
    grad_attn = jnp.concatenate(pieces, axis=0)
    grad_rows = times_rows(grad_attn, out_w).astype(bf16)
    grad_heads = grad_rows.reshape(tok_rows, heads_local, HD).transpose(1, 0, 2).reshape(-1, HD)
    grad_q, pair_grad = attend_back(
        query_rows, grad_heads, attn_float, attn_log, pairs, places, key_places
    )
    if gather_factors:
        pair_grad = after(pair_grad, own_columns)
        columns_then = after(own_columns, grad_attn)
        if layers == 4:
            column_pieces = [columns_then] + [swap(columns_then, bit, "tp") for bit in (1, 2)]
        else:
            column_pieces, _, _ = layer_gather(columns_then)
    near_rows = 4 * tok_rows
    pair_part = [
        pair_grad[start : start + near_rows] for start in range(0, key_count, near_rows)
    ]
    for bit in reversed(near):
        half = len(pair_part) // 2
        pair_part = [
            (kept.astype(f32) + swap(sent, bit).astype(f32)).astype(bf16)
            for kept, sent in zip(pair_part[:half], pair_part[half:])
        ]
    pair_part = pair_part[0]
    if layers == 4:
        output_pieces.append(swap(after(output_pieces[2], grad_rows), 1, "tp"))
    arrived = [
        swap(pair_part[index * tok_rows : (index + 1) * tok_rows], step)
        for index, step in ((1, far_a), (2, far_b), (3, far_a | far_b))
    ]
    pair_own = after(pair_part[:tok_rows], output_pieces[3]).astype(f32)
    for piece in arrived:
        pair_own = pair_own + piece.astype(f32)
    if gather_factors:
        if layers == 4:
            column_pieces.append(swap(after(column_pieces[2], arrived[0]), 1, "tp"))
    grad_query_lin = (
        rotate(
            grad_q.reshape(heads_local, tok_rows, HD).transpose(1, 0, 2), cos_table, -sine_table
        )
        * HD ** (-0.5)
    ).reshape(tok_rows, query_width)
    grad_key_lin = rotate(
        pair_own[:, :key_width].reshape(tok_rows, key_heads, HD), cos_table, -sine_table
    ).reshape(tok_rows, key_width)
    grad_lin = jnp.concatenate(
        [grad_query_lin, grad_key_lin, pair_own[:, key_width:]], axis=1
    ).astype(bf16)
    partial = attn_products(
        attn_input,
        after(grad_lin, all_both) if gather_factors else grad_lin,
        grad_attn,
        attn_rows,
    )
    attn_sums = sum_scatter(partial)
    grad_w_lin, grad_w_out = attn_sums[:, :qkv_width], attn_sums[:, qkv_width:]
    grad_in_part = times_rows_t(after(grad_lin, partial), qkv_w).astype(bf16)

    if gather_factors:
        columns = jnp.stack([after(piece, grad_in_part) for piece in column_pieces], axis=1)
        columns = columns.reshape(tok_rows * ring, 2 * shard)
        ffn_cols, down_cols = columns[:, :shard], columns[:, shard:]

    def gate_gradient(then):
        return (contract(after(ffn_cols, then), all_both[:, :ffn_width], 0, 0),)

    if gather_factors:
        parts, _, (grad_w_gate,) = layer_scatter(grad_in_part, None, gate_gradient)
    else:
        parts, _, _ = layer_scatter(grad_in_part)
    if in_kernels:
        own_grad, grad_gain_one = on_own_rows(
            token_back_body,
            *parts,
            (own_tok, grad_res, all_gains),
            [(own_rows, bf16), (1, f32)],
            "token_back",
            scratch=2,
        )
    else:
        grad_attn_in = columns_out(sum_of(parts))
        own_inv = rms_scale(own_tok)
        own_normed = own_tok * own_inv
        own_grad = grad_res + norm_back(own_inv, own_normed, grad_attn_in * gain_one)
        own_grad = own_grad.astype(bf16)
        grad_gain_one = jnp.sum(grad_attn_in * own_normed, axis=0, keepdims=True)
    token_pieces, _, _ = layer_gather(own_grad)
    if gather_factors:
        grad_w_up = contract(after(ffn_cols, own_grad), all_both[:, ffn_width:], 0, 0)
    grad_tokens = rows_out(token_pieces).astype(f32)
    output = rows_out([after(output_pieces[0], own_grad)] + output_pieces[1:])

    third_gain = norm_ffn_in.astype(f32)
    gain_third = (
        jnp.sum(w_gate.astype(f32) * grad_w_gate + w_up.astype(f32) * grad_w_up, axis=1)
        / third_gain
    )[None, :]
    gain_sum = columns_in(
        jnp.concatenate([grad_gain_one, grad_gain_two, grad_gain_four], axis=0)
    )
    gain_sum = after(gain_sum, token_pieces[1])
    for bit in reversed(near):
        half = gain_sum.shape[1] // 2
        gain_sum = gain_sum[:, :half] + swap(gain_sum[:, half:], bit)
    own_gain = gain_sum[:, :shard]
    for index, step in ((1, far_a), (2, far_b), (3, far_a | far_b)):
        own_gain = own_gain + swap(gain_sum[:, index * shard : (index + 1) * shard], step)
    own_gain = jnp.concatenate([own_gain, gain_third], axis=0)
    for piece in [swap(own_gain, step, "tp") for step in range(1, layers)]:
        own_gain = own_gain + piece
    if gather_factors:
        grad_w_down = contract(after(down_cols, own_gain), all_hidden, 0, 0)
    return (
        output,
        grad_tokens,
        grad_w_lin[:, :query_width],
        grad_w_lin[:, query_width : query_width + key_width],
        grad_w_lin[:, query_width + key_width :],
        grad_w_out,
        grad_w_gate,
        grad_w_up,
        grad_w_down,
        own_gain[0],
        own_gain[1],
        own_gain[3],
        own_gain[2],
    )


def solution(mesh):
    rows, block = P("ctx", None), P("ctx", "tp")
    gain = P("ctx")
    return jax.shard_map(
        local,
        mesh=mesh,
        in_specs=(rows,) + (block,) * 7 + (gain,) * 4 + (rows,),
        out_specs=(rows, rows) + (block,) * 7 + (gain,) * 4,
        check_vma=False,
    )
```

```python
import functools
import math

import jax
import jax.numpy as jnp
from jax import lax
from jax.experimental import pallas as pl
from jax.experimental.pallas import tpu as pltpu
from jax.sharding import PartitionSpec as P

HD = 256


EPSILON = 1e-06
SOFT_CAP = 50.0
MASKED = -1e30

bf16, f32 = jnp.bfloat16, jnp.float32


def rms_scale(values):
    return lax.rsqrt(jnp.mean(values * values, axis=-1, keepdims=True) + EPSILON)


def norm_back(inv_rms, normed, gradient):
    return inv_rms * (gradient - normed * jnp.mean(gradient * normed, axis=-1, keepdims=True))


def rotate(values, cos_table, sine_table):
    half_width = values.shape[-1] // 2
    leading = values[..., :half_width]
    trailing = values[..., half_width:]
    return jnp.concatenate(
        [leading * cos_table - trailing * sine_table, trailing * cos_table + leading * sine_table],
        axis=-1,
    )


def gelu_tanh(values):
    return jax.nn.gelu(values, approximate=True)


def product(first_operand, second_operand):
    return jnp.dot(first_operand, second_operand, preferred_element_type=f32)


def contract(first_operand, second_operand, first_dim, second_dim):
    return lax.dot_general(
        first_operand,
        second_operand,
        (((first_dim,), (second_dim,)), ((), ())),
        preferred_element_type=f32,
    )


def after(value, *earlier):
    return lax.optimization_barrier((value,) + earlier)[0]


def swap(value, bit, axis="ctx"):
    count = lax.axis_size(axis)
    return lax.ppermute(value, axis, [(index, index ^ bit) for index in range(count)])


WHOLE = pl.BlockSpec(memory_space=pltpu.VMEM)
SCALARS = pl.BlockSpec(memory_space=pltpu.SMEM)
VMEM_BYTES = 24 * 2**20


def shape_of(dims, kind):
    return jax.ShapeDtypeStruct(dims, kind)


def key_block(key_count):
    return math.gcd(key_count, 512)


def attend_kernel(steps, group, query_ref, pair_ref, place_ref, key_place_ref, out_ref, rows_ref, log_ref):
    step = pl.program_id(0)
    rows = place_ref.shape[0]

    @pl.when(step == 0)
    def _():
        out_ref[...] = jnp.zeros_like(out_ref)
        log_ref[...] = jnp.zeros_like(log_ref)

    keys, values = pair_ref[:, :HD], pair_ref[:, HD:]
    scores = contract(query_ref[...], keys, 1, 1)
    capped = SOFT_CAP * jnp.tanh(scores * (1.0 / SOFT_CAP))
    visible = key_place_ref[...] <= place_ref[...]
    weights = jnp.where(visible, jnp.exp(capped), 0.0)
    log_ref[...] += jnp.sum(weights, axis=-1, keepdims=True)
    out_ref[...] += product(weights.astype(bf16), values)

    @pl.when(step == steps - 1)
    def _():
        total = log_ref[...]
        result = out_ref[...] / total
        out_ref[...] = result
        log_ref[...] = jnp.log(total)
        each = rows // group
        for head in range(group):
            rows_ref[:, head * HD : (head + 1) * HD] = result[head * each : (head + 1) * each].astype(bf16)


def attend(queries, pairs, places, key_places, group):
    rows, key_count = queries.shape[0], pairs.shape[0]
    block = key_block(key_count)
    steps = key_count // block
    fixed = lambda step: (0, 0)
    return pl.pallas_call(
        functools.partial(attend_kernel, steps, group),
        grid=(steps,),
        in_specs=[
            pl.BlockSpec((rows, HD), fixed),
            pl.BlockSpec((block, 2 * HD), lambda step: (step, 0)),
            pl.BlockSpec((rows, 1), fixed),
            pl.BlockSpec((1, block), lambda step: (0, step)),
        ],
        out_specs=[
            pl.BlockSpec((rows, HD), fixed),
            pl.BlockSpec((rows // group, group * HD), fixed),
            pl.BlockSpec((rows, 1), fixed),
        ],
        out_shape=[
            shape_of((rows, HD), f32),
            shape_of((rows // group, group * HD), bf16),
            shape_of((rows, 1), f32),
        ],
        compiler_params=pltpu.CompilerParams(vmem_limit_bytes=VMEM_BYTES),
        name="attend",
    )(queries, pairs, places, key_places)


def attend_back_kernel(
    steps, query_ref, grad_ref, out_ref, log_ref, pair_ref, place_ref, key_place_ref, query_grad_ref, own_ref, near_ref, delta_ref
):
    @pl.when(pl.program_id(0) == 0)
    def _():
        query_grad_ref[...] = jnp.zeros_like(query_grad_ref)
        delta_ref[...] = jnp.sum(grad_ref[...].astype(f32) * out_ref[...], axis=-1, keepdims=True)

    queries, grads = query_ref[...], grad_ref[...]
    keys, values = pair_ref[:, :HD], pair_ref[:, HD:]
    part = jnp.tanh(contract(queries, keys, 1, 1) * (1.0 / SOFT_CAP))
    visible = key_place_ref[...] <= place_ref[...]
    probs = jnp.where(visible, jnp.exp(SOFT_CAP * part - log_ref[...]), 0.0)
    value_grad = contract(probs.astype(bf16), grads, 0, 0).astype(bf16)
    slope = contract(grads, values, 1, 1) - delta_ref[...]
    score_grad = (probs * slope * (1.0 - part * part)).astype(bf16)
    query_grad_ref[...] += product(score_grad, keys)
    key_grad = contract(score_grad, queries, 0, 0).astype(bf16)

    @pl.when(pl.program_id(0) < steps // 2)
    def _():
        own_ref[:, :HD] = key_grad
        own_ref[:, HD:] = value_grad

    @pl.when(pl.program_id(0) >= steps // 2)
    def _():
        near_ref[:, :HD] = key_grad
        near_ref[:, HD:] = value_grad


def attend_back(queries, grads, outs, logs, pairs, places, key_places):
    rows, key_count = queries.shape[0], pairs.shape[0]
    block = key_block(key_count)
    fixed = lambda step: (0, 0)
    tall = pl.BlockSpec((rows, HD), fixed)
    column = pl.BlockSpec((rows, 1), fixed)
    moving = pl.BlockSpec((block, 2 * HD), lambda step: (step, 0))
    steps = key_count // block
    first = pl.BlockSpec((block, 2 * HD), lambda step: (jnp.minimum(step, steps // 2 - 1), 0))
    second = pl.BlockSpec((block, 2 * HD), lambda step: (jnp.maximum(step - steps // 2, 0), 0))
    half = shape_of((key_count // 2, 2 * HD), bf16)
    return pl.pallas_call(
        functools.partial(attend_back_kernel, steps),
        grid=(steps,),
        in_specs=[tall, tall, tall, column, moving, column, pl.BlockSpec((1, block), lambda step: (0, step))],
        out_specs=[tall, first, second],
        out_shape=[shape_of((rows, HD), f32), half, half],
        scratch_shapes=[pltpu.VMEM((rows, 1), f32)],
        compiler_params=pltpu.CompilerParams(vmem_limit_bytes=VMEM_BYTES),
        name="attend_back",
    )(queries, grads, outs, logs, pairs, places, key_places)


def local(
    tokens,
    w_query,
    w_key,
    w_value,
    w_out,
    w_gate,
    w_up,
    w_down,
    norm_attn_in,
    norm_attn_out,
    norm_ffn_in,
    norm_ffn_out,
    cotangent,
):
    tok_rows, width = tokens.shape
    heads_local = w_query.shape[1] // HD
    key_heads = w_key.shape[1] // HD
    query_width = heads_local * HD
    key_width = key_heads * HD
    qkv_width = query_width + 2 * key_width
    ffn_width = w_gate.shape[1]
    ring = lax.axis_size("ctx")
    layers = lax.axis_size("tp")
    me = lax.axis_index("ctx")
    my_layer = lax.axis_index("tp")
    shard = width // ring
    own_rows = tok_rows // layers
    upper = shard // 32 * 16
    far_a, far_b = ring // 4, ring // 2
    near = [1 << bit for bit in range(far_a.bit_length() - 1)]
    order = [0, far_a, far_b, far_a | far_b]
    for bit in near:
        order = order + [block | bit for block in order]
    near_width = 4 * shard
    gather_factors = tok_rows * ring <= width

    def spread_far(piece):
        from_a, from_b = swap(piece, far_a), swap(piece, far_b)
        return from_a, from_b, swap(from_b[:upper], far_a), swap(from_a[upper:shard], far_b)

    def spread_near(block):
        blocks = [block]
        for bit in near:
            blocks = blocks + [swap(held, bit) for held in blocks]
        return blocks

    def by_near(array):
        return [array[:, start : start + near_width] for start in range(0, width, near_width)]

    def times_rows(activation, blocks):
        total = None
        for part, block in zip(by_near(activation), blocks):
            term = product(part, block)
            total = term if total is None else total + term
        return total

    def times_rows_t(activation, blocks):
        return jnp.concatenate([contract(activation, block, 1, 1) for block in blocks], axis=1)

    def layer_scatter(partial, first=None, second=None):
        pieces = [partial[step * own_rows : (step + 1) * own_rows] for step in range(layers)]
        done_first = first(partial) if first else ()
        if layers == 4:
            passed_on = swap(pieces[3], 1, "tp")
            arrived = [swap(pieces[1], 1, "tp")]
            held = after(pieces[2], *done_first) if first else pieces[2]
            pair_sum = (held.astype(f32) + passed_on.astype(f32)).astype(bf16)
            arrived.append(swap(pair_sum, 2, "tp"))
        else:
            pair_sum = partial
            arrived = [swap(pieces[step], step, "tp") for step in range(1, layers)]
        done_second = second(pair_sum) if second else ()
        if done_first or done_second:
            arrived[0] = after(arrived[0], *done_first, *done_second)
        return (partial, arrived), done_first, done_second

    def sum_of(parts):
        partial, arrived = parts
        total = partial[:own_rows].astype(f32)
        for piece in arrived:
            total = total + piece.astype(f32)
        return total

    def layer_gather(rows, first=None, second=None):
        done_first = first(rows) if first else ()
        if layers == 4:
            across = swap(rows, 2, "tp")
            beside = swap(rows, 1, "tp")
            across_then = after(across, *done_first) if first else across
            pieces = [rows, beside, across, swap(across_then, 1, "tp")]
        else:
            across_then = rows
            pieces = [rows] + [swap(rows, step, "tp") for step in range(1, layers)]
        done_second = second(across_then) if second else ()
        if first or second:
            pieces[0] = after(pieces[0], *done_first, *done_second)
        return pieces, done_first, done_second

    def rows_in(array):
        return jnp.concatenate(
            [
                lax.dynamic_slice_in_dim(array, (my_layer ^ step) * own_rows, own_rows, 0)
                for step in range(layers)
            ],
            axis=0,
        )

    def rows_out(pieces):
        result = jnp.zeros((tok_rows,) + pieces[0].shape[1:], pieces[0].dtype)
        for step, piece in enumerate(pieces):
            result = lax.dynamic_update_slice_in_dim(
                result, piece, (my_layer ^ step) * own_rows, 0
            )
        return result

    def columns_in(array):
        return jnp.concatenate(
            [lax.dynamic_slice_in_dim(array, (me ^ block) * shard, shard, 1) for block in order],
            axis=1,
        )

    def columns_out(array):
        def place(block):
            found = (block & far_a) // far_a + 2 * ((block & far_b) // far_b)
            for index, bit in enumerate(near):
                found = found + (4 << index) * ((block & bit) // bit)
            return found

        return jnp.concatenate(
            [
                lax.dynamic_slice_in_dim(array, place(me ^ block) * shard, shard, 1)
                for block in range(ring)
            ],
            axis=1,
        )

    def rows_of_all(array):
        return lax.all_gather(array, "ctx", axis=0, tiled=True)

    def in_order(me_ref, source_ref, target_ref, inverse):
        for index in range(ring):

            @pl.when(me_ref[0] == index)
            def _():
                for place, block in enumerate(order):
                    here = slice(place * shard, (place + 1) * shard)
                    there = slice((index ^ block) * shard, ((index ^ block) + 1) * shard)
                    if inverse:
                        target_ref[:, there] = source_ref[:, here]
                    else:
                        target_ref[:, here] = source_ref[:, there]

    in_kernels = ring <= 8 and own_rows % 16 == 0 and layers == 4

    def on_own_rows(body, partial, arrived, others, outs, name, scratch=1):
        def kernel(me_ref, part_ref, one_ref, two_ref, *refs):
            total = part_ref[...].astype(f32) + one_ref[...].astype(f32) + two_ref[...].astype(f32)
            body(me_ref, total, *refs)

        wide = pl.BlockSpec((own_rows, width), lambda step: (0, 0))
        return pl.pallas_call(
            kernel,
            grid=(1,),
            in_specs=[SCALARS, wide] + [WHOLE] * (2 + len(others)),
            out_specs=[WHOLE] * len(outs),
            out_shape=[shape_of((rows, width), kind) for rows, kind in outs],
            scratch_shapes=[pltpu.VMEM((own_rows, width), f32)] * scratch,
            compiler_params=pltpu.CompilerParams(vmem_limit_bytes=VMEM_BYTES),
            name=name,
        )(me[None], partial, *arrived, *others)

    def residual_body(me_ref, total, tok_ref, gain_ref, attn_ref, hidden_ref, input_ref, held_ref):
        held_ref[...] = total
        in_order(me_ref, held_ref, attn_ref, True)
        attn = attn_ref[...]
        hidden = tok_ref[...] + attn * rms_scale(attn) * gain_ref[0:1, :]
        hidden_ref[...] = hidden
        input_ref[...] = (hidden * rms_scale(hidden) * gain_ref[1:2, :]).astype(bf16)

    def output_body(me_ref, total, hidden_ref, cot_ref, gain_ref, out_ref, grad_ref, gain_grad_ref):
        inverse = rms_scale(total)
        normed = total * inverse
        gain, cot = gain_ref[2:3, :], cot_ref[...]
        out_ref[...] = (hidden_ref[...] + normed * gain).astype(bf16)
        gain_grad_ref[...] = jnp.sum(cot * normed, axis=0, keepdims=True)
        grad_ref[...] = norm_back(inverse, normed, cot * gain).astype(bf16)

    def residual_back_body(
        me_ref, total, hidden_ref, attn_ref, cot_ref, gain_ref, res_ref, grad_ref, gain_grad_ref, held_ref, moved_ref
    ):
        hidden, attn = hidden_ref[...], attn_ref[...]
        inverse = rms_scale(hidden)
        res = cot_ref[...] + norm_back(inverse, hidden * inverse, total * gain_ref[1:2, :])
        res_ref[...] = res
        inverse = rms_scale(attn)
        normed = attn * inverse
        gain_grad_ref[...] = jnp.sum(res * normed, axis=0, keepdims=True)
        held_ref[...] = norm_back(inverse, normed, res * gain_ref[0:1, :])
        in_order(me_ref, held_ref, moved_ref, False)
        grad_ref[...] = moved_ref[...].astype(bf16)

    def token_back_body(me_ref, total, tok_ref, res_ref, gain_ref, grad_ref, gain_grad_ref, held_ref, moved_ref):
        held_ref[...] = total
        in_order(me_ref, held_ref, moved_ref, True)
        tok, grad = tok_ref[...], moved_ref[...]
        inverse = rms_scale(tok)
        normed = tok * inverse
        gain_grad_ref[...] = jnp.sum(grad * normed, axis=0, keepdims=True)
        grad_ref[...] = (
            res_ref[...] + norm_back(inverse, normed, grad * gain_ref[3:4, :])
        ).astype(bf16)

    def by_owner_kernel(first_ref, second_ref, out_ref):
        for block in range(ring):
            here = slice(block * shard, (block + 1) * shard)
            out_ref[block, :, :shard] = first_ref[:, here]
            out_ref[block, :, shard:] = second_ref[:, here]

    def columns_by_owner(first, second):
        rows = first.shape[0]
        if not in_kernels:
            stacked = jnp.stack([array.reshape(rows, ring, shard) for array in (first, second)])
            return stacked.transpose(2, 1, 0, 3).reshape(ring, rows, 2 * shard)
        return pl.pallas_call(
            by_owner_kernel,
            in_specs=[WHOLE] * 2,
            out_specs=WHOLE,
            out_shape=shape_of((ring, rows, 2 * shard), bf16),
            compiler_params=pltpu.CompilerParams(vmem_limit_bytes=VMEM_BYTES),
            name="by_owner",
        )(first, second)

    def sum_scatter(partial):
        return lax.psum_scatter(
            partial.astype(bf16), "ctx", scatter_dimension=0, tiled=True
        ).astype(f32)

    def products_kernel(me_ref, input_ref, lin_ref, grad_ref, rows_ref, out_ref):
        for place, block in enumerate(order):
            rows = pl.ds(pl.multiple_of((me_ref[0] ^ block) * shard, 16), shard)
            here = slice(place * shard, (place + 1) * shard)
            out_ref[rows, :qkv_width] = contract(input_ref[:, here], lin_ref[...], 0, 0).astype(bf16)
            out_ref[rows, qkv_width:] = contract(grad_ref[:, here], rows_ref[...], 0, 0).astype(bf16)

    def attn_products(inputs, lin, grads, rows):
        if shard % 16:
            return jnp.concatenate(
                [
                    contract(columns_out(inputs), lin, 0, 0),
                    contract(columns_out(grads), rows, 0, 0),
                ],
                axis=1,
            ).astype(bf16)
        return pl.pallas_call(
            products_kernel,
            in_specs=[SCALARS] + [WHOLE] * 4,
            out_specs=WHOLE,
            out_shape=shape_of((width, qkv_width + query_width), bf16),
            compiler_params=pltpu.CompilerParams(vmem_limit_bytes=56 * 2**20),
            name="attn_products",
        )(me[None], inputs, lin, grads, rows)

    gate_up = rows_of_all(jnp.concatenate([w_gate, w_up], axis=1))
    down_w = rows_of_all(w_down)
    attn_own = jnp.concatenate([w_query, w_key, w_value, w_out], axis=1)
    own_gains = jnp.stack([norm_attn_out, norm_ffn_in, norm_ffn_out, norm_attn_in])
    gain_rows = jnp.zeros((16, attn_own.shape[1]), bf16).at[:4, :shard].set(own_gains)
    from_a, from_b, top, bottom = spread_far(jnp.concatenate([attn_own, gain_rows], axis=0))
    attn_w = spread_near(
        jnp.concatenate([attn_own, from_a[:shard], from_b[:shard], top, bottom], axis=0)
    )
    qkv_w = [block[:, :qkv_width] for block in attn_w]
    out_w = [block[:, qkv_width:] for block in attn_w]
    gain_a, gain_b = (held[shard : shard + 4, :shard] for held in (from_a, from_b))
    gains = jnp.concatenate(
        spread_near(
            jnp.concatenate([own_gains, gain_a, gain_b, swap(gain_b, far_a)], axis=1)
        ),
        axis=1,
    )
    all_gains = columns_out(gains).astype(f32)
    gain_two, gain_three, gain_four, gain_one = jnp.split(all_gains, 4)

    tok_float = rows_in(tokens).astype(f32)
    own_cot = lax.dynamic_slice_in_dim(cotangent, my_layer * own_rows, own_rows, 0).astype(f32)
    own_tok = tok_float[:own_rows]
    attn_input = lax.optimization_barrier(
        (
            columns_in(rows_in(tokens)).astype(f32) * rms_scale(tok_float) * gains[3:].astype(f32)
        ).astype(bf16)
    )
    lin = times_rows(attn_input, qkv_w)
    row_place = jnp.concatenate(
        [
            (my_layer ^ step) * own_rows + jnp.arange(own_rows, dtype=jnp.int32)
            for step in range(layers)
        ]
    )
    query_pos = me * tok_rows + row_place
    half_width = HD // 2
    frequency = jnp.exp(jnp.arange(half_width, dtype=f32) * (-2.0 * math.log(10000.0) / HD))
    angles = query_pos.astype(f32)[:, None] * frequency[None, :]
    cos_table, sine_table = jnp.cos(angles)[:, None, :], jnp.sin(angles)[:, None, :]
    queries = (
        rotate(lin[:, :query_width].reshape(tok_rows, heads_local, HD), cos_table, sine_table)
        * HD ** (-0.5)
    ).astype(bf16)
    assert key_heads == 1
    query_rows = queries.reshape(tok_rows, heads_local, HD).transpose(1, 0, 2).reshape(-1, HD)
    keys_rot = (
        rotate(
            lin[:, query_width : query_width + key_width].reshape(tok_rows, key_heads, HD),
            cos_table,
            sine_table,
        )
        .astype(bf16)
        .reshape(tok_rows, key_width)
    )
    values_b = lin[:, query_width + key_width :].astype(bf16)
    pair = jnp.concatenate([keys_rot, values_b], axis=1)
    pair_far = jnp.concatenate(
        [pair] + [swap(pair, step) for step in (far_a, far_b, far_a | far_b)], axis=0
    )
    pairs = jnp.concatenate(spread_near(pair_far), axis=0)
    key_count = pairs.shape[0]
    key_places = jnp.concatenate([(me ^ block) * tok_rows + row_place for block in order])[None, :]
    places = jnp.tile(query_pos, heads_local)[:, None]
    attn_float, attn_rows, attn_log = attend(query_rows, pairs, places, key_places, heads_local)
    parts, _, _ = layer_scatter(times_rows_t(attn_rows, out_w).astype(bf16))
    if in_kernels:
        attn_total, hidden_res, own_input = on_own_rows(
            residual_body,
            *parts,
            (own_tok, all_gains),
            [(own_rows, f32), (own_rows, f32), (own_rows, bf16)],
            "residual",
        )
    else:
        attn_total = columns_out(sum_of(parts))
        hidden_res = own_tok + attn_total * rms_scale(attn_total) * gain_two
        own_input = (hidden_res * rms_scale(hidden_res) * gain_three).astype(bf16)
    pieces, _, _ = layer_gather(own_input)
    ffn_input = jnp.concatenate(pieces, axis=0)

    both_lin = product(ffn_input, gate_up)
    gate_lin, up_lin = both_lin[:, :ffn_width], both_lin[:, ffn_width:]
    activated, gelu_pull = jax.vjp(gelu_tanh, gate_lin)
    hidden_b = (activated * up_lin).astype(bf16)
    if gather_factors:
        all_hidden = rows_of_all(hidden_b)
    parts, _, _ = layer_scatter(contract(hidden_b, down_w, 1, 1).astype(bf16))
    if in_kernels:
        own_output, own_grad_ffn, grad_gain_four = on_own_rows(
            output_body,
            *parts,
            (hidden_res, own_cot, all_gains),
            [(own_rows, bf16), (own_rows, bf16), (1, f32)],
            "output",
            scratch=0,
        )
    else:
        ffn_total = sum_of(parts)
        inv_four = rms_scale(ffn_total)
        normed_four = ffn_total * inv_four
        own_output = (hidden_res + normed_four * gain_four).astype(bf16)
        grad_gain_four = jnp.sum(own_cot * normed_four, axis=0, keepdims=True)
        own_grad_ffn = norm_back(inv_four, normed_four, own_cot * gain_four).astype(bf16)

    pieces, _, _ = layer_gather(own_grad_ffn)
    grad_ffn = jnp.concatenate(pieces, axis=0)
    if gather_factors:
        own_columns = lax.all_to_all(
            columns_by_owner(own_input, own_grad_ffn),
            "ctx",
            split_axis=0,
            concat_axis=0,
            tiled=True,
        )
    sent_output = after(own_output, grad_ffn)
    if layers == 4:
        output_pieces = [own_output, swap(sent_output, 1, "tp"), swap(sent_output, 2, "tp")]
    else:
        output_pieces, _, _ = layer_gather(sent_output)
    grad_hidden = product(grad_ffn, down_w)
    grad_gate = gelu_pull(grad_hidden * up_lin)[0].astype(bf16)
    grad_up = (grad_hidden * activated).astype(bf16)
    grad_both = jnp.concatenate([grad_gate, grad_up], axis=1)
    if gather_factors:
        all_both = rows_of_all(after(grad_both, all_hidden))
    else:
        grad_w_down = sum_scatter(contract(grad_ffn, hidden_b, 0, 0))
        grad_w_both = sum_scatter(contract(ffn_input, grad_both, 0, 0))
        grad_w_gate, grad_w_up = grad_w_both[:, :ffn_width], grad_w_both[:, ffn_width:]
    grad_in_part = contract(grad_both, gate_up, 1, 1).astype(bf16)
    grad_in_part = after(grad_in_part, *output_pieces[1:])
    parts, _, _ = layer_scatter(grad_in_part)
    if in_kernels:
        grad_res, own_grad_attn, grad_gain_two = on_own_rows(
            residual_back_body,
            *parts,
            (hidden_res, attn_total, own_cot, all_gains),
            [(own_rows, f32), (own_rows, bf16), (1, f32)],
            "residual_back",
            scratch=2,
        )
    else:
        inv_three = rms_scale(hidden_res)
        grad_res = own_cot + norm_back(
            inv_three, hidden_res * inv_three, sum_of(parts) * gain_three
        )
        inv_two = rms_scale(attn_total)
        normed_two = attn_total * inv_two
        grad_gain_two = jnp.sum(grad_res * normed_two, axis=0, keepdims=True)
        own_grad_attn = norm_back(inv_two, normed_two, grad_res * gain_two)
        own_grad_attn = columns_in(own_grad_attn.astype(bf16))

    pieces, _, _ = layer_gather(own_grad_attn)
    grad_attn = jnp.concatenate(pieces, axis=0)
    grad_rows = times_rows(grad_attn, out_w).astype(bf16)
    grad_heads = grad_rows.reshape(tok_rows, heads_local, HD).transpose(1, 0, 2).reshape(-1, HD)
    grad_q, *pair_halves = attend_back(
        query_rows, grad_heads, attn_float, attn_log, pairs, places, key_places
    )
    if gather_factors:
        pair_halves = [after(half, own_columns) for half in pair_halves]
        columns_then = after(own_columns, grad_attn)
        if layers == 4:
            column_pieces = [columns_then] + [swap(columns_then, bit, "tp") for bit in (1, 2)]
        else:
            column_pieces, _, _ = layer_gather(columns_then)
    near_rows = 4 * tok_rows
    pair_part = [
        half[start : start + near_rows]
        for half in pair_halves
        for start in range(0, half.shape[0], near_rows)
    ]
    for bit in reversed(near):
        half = len(pair_part) // 2
        pair_part = [
            (kept.astype(f32) + swap(sent, bit).astype(f32)).astype(bf16)
            for kept, sent in zip(pair_part[:half], pair_part[half:])
        ]
    pair_part = pair_part[0]
    if layers == 4:
        output_pieces.append(swap(after(output_pieces[2], grad_rows), 1, "tp"))
    arrived = [
        swap(pair_part[index * tok_rows : (index + 1) * tok_rows], step)
        for index, step in ((1, far_a), (2, far_b), (3, far_a | far_b))
    ]
    pair_own = after(pair_part[:tok_rows], output_pieces[3]).astype(f32)
    for piece in arrived:
        pair_own = pair_own + piece.astype(f32)
    if gather_factors:
        if layers == 4:
            column_pieces.append(swap(after(column_pieces[2], arrived[0]), 1, "tp"))
    grad_query_lin = (
        rotate(
            grad_q.reshape(heads_local, tok_rows, HD).transpose(1, 0, 2), cos_table, -sine_table
        )
        * HD ** (-0.5)
    ).reshape(tok_rows, query_width)
    grad_key_lin = rotate(
        pair_own[:, :key_width].reshape(tok_rows, key_heads, HD), cos_table, -sine_table
    ).reshape(tok_rows, key_width)
    grad_lin = jnp.concatenate(
        [grad_query_lin, grad_key_lin, pair_own[:, key_width:]], axis=1
    ).astype(bf16)
    partial = attn_products(
        attn_input,
        after(grad_lin, all_both) if gather_factors else grad_lin,
        grad_attn,
        attn_rows,
    )
    attn_sums = sum_scatter(partial)
    grad_w_lin, grad_w_out = attn_sums[:, :qkv_width], attn_sums[:, qkv_width:]
    grad_in_part = times_rows_t(after(grad_lin, partial), qkv_w).astype(bf16)

    if gather_factors:
        columns = jnp.stack([after(piece, grad_in_part) for piece in column_pieces], axis=1)
        columns = columns.reshape(tok_rows * ring, 2 * shard)
        ffn_cols, down_cols = columns[:, :shard], columns[:, shard:]

    def gate_gradient(then):
        return (contract(after(ffn_cols, then), all_both[:, :ffn_width], 0, 0),)

    if gather_factors:
        parts, _, (grad_w_gate,) = layer_scatter(grad_in_part, None, gate_gradient)
    else:
        parts, _, _ = layer_scatter(grad_in_part)
    if in_kernels:
        own_grad, grad_gain_one = on_own_rows(
            token_back_body,
            *parts,
            (own_tok, grad_res, all_gains),
            [(own_rows, bf16), (1, f32)],
            "token_back",
            scratch=2,
        )
    else:
        grad_attn_in = columns_out(sum_of(parts))
        own_inv = rms_scale(own_tok)
        own_normed = own_tok * own_inv
        own_grad = grad_res + norm_back(own_inv, own_normed, grad_attn_in * gain_one)
        own_grad = own_grad.astype(bf16)
        grad_gain_one = jnp.sum(grad_attn_in * own_normed, axis=0, keepdims=True)
    token_pieces, _, _ = layer_gather(own_grad)
    if gather_factors:
        grad_w_up = contract(after(ffn_cols, own_grad), all_both[:, ffn_width:], 0, 0)
    grad_tokens = rows_out(token_pieces).astype(f32)
    output = rows_out([after(output_pieces[0], own_grad)] + output_pieces[1:])

    third_gain = norm_ffn_in.astype(f32)
    gain_third = (
        jnp.sum(w_gate.astype(f32) * grad_w_gate + w_up.astype(f32) * grad_w_up, axis=1)
        / third_gain
    )[None, :]
    gain_sum = columns_in(
        jnp.concatenate([grad_gain_one, grad_gain_two, grad_gain_four], axis=0)
    )
    gain_sum = after(gain_sum, token_pieces[1])
    for bit in reversed(near):
        half = gain_sum.shape[1] // 2
        gain_sum = gain_sum[:, :half] + swap(gain_sum[:, half:], bit)
    own_gain = gain_sum[:, :shard]
    for index, step in ((1, far_a), (2, far_b), (3, far_a | far_b)):
        own_gain = own_gain + swap(gain_sum[:, index * shard : (index + 1) * shard], step)
    own_gain = jnp.concatenate([own_gain, gain_third], axis=0)
    for piece in [swap(own_gain, step, "tp") for step in range(1, layers)]:
        own_gain = own_gain + piece
    if gather_factors:
        grad_w_down = contract(after(down_cols, own_gain), all_hidden, 0, 0)
    return (
        output,
        grad_tokens,
        grad_w_lin[:, :query_width],
        grad_w_lin[:, query_width : query_width + key_width],
        grad_w_lin[:, query_width + key_width :],
        grad_w_out,
        grad_w_gate,
        grad_w_up,
        grad_w_down,
        own_gain[0],
        own_gain[1],
        own_gain[3],
        own_gain[2],
    )


def solution(mesh):
    rows, block = P("ctx", None), P("ctx", "tp")
    gain = P("ctx")
    return jax.shard_map(
        local,
        mesh=mesh,
        in_specs=(rows,) + (block,) * 7 + (gain,) * 4 + (rows,),
        out_specs=(rows, rows) + (block,) * 7 + (gain,) * 4,
        check_vma=False,
    )
```
